512 devices in a mesh: group: 16 (over z, core), dom: 32 (over y, x).
Axes of the slice: x: 4, y: 8, z: 8, core: 2. Of those that a mesh axis runs over, the one named last changes fastest.
Arguments:
- queries: bfloat16 [131072, 512], P(('group', 'dom')), may hold values from -8 to 8
- keys: bfloat16 [131072, 512], P(('group', 'dom')), may hold values from -8 to 8
- values: bfloat16 [131072, 512], P(('group', 'dom')), may hold values from -6 to 6
- cotangent: bfloat16 [131072, 512], P(('group', 'dom')), may hold values from -6 to 6
- local_list: int32 [1024, 3], P('group'), may hold values from 0 to 63, as said below
- far_list: int32 [32, 32, 3], P('dom'), may hold values from 0 to 31, as said below
Outputs:
- attended: bfloat16 [131072, 512], P(('group', 'dom'))
- grad_queries: bfloat16 [131072, 512], P(('group', 'dom'))
- grad_keys: bfloat16 [131072, 512], P(('group', 'dom'))
- grad_values: bfloat16 [131072, 512], P(('group', 'dom'))
The draws below stay inside these ranges and needn't reach their ends.
Inputs may be any that keep to these rules, and one draw needn't show every extreme that they name: `local_list`: an entry names a block of the query block's own cluster held by the same device or by a device at most 2 places away along dom. Over the 2 query blocks of one device, the entries name exactly one block of each other device within that reach; devices with fewer than 2 neighbours on a side list their own blocks in those places. Row g * 2 + s of far_list[d] belongs to query block (g, d, s); an entry v names slot v % 2 of the device at position d of cluster v // 2, never cluster g. Over the 2 query blocks of one device, at most one distinct block of each other cluster is named.
All inputs are finite; a program needn't handle non-finite values.
Results may differ from the reference program's by a relative error of at most 0.012.
The reference program's roundings to bfloat16 on the way count: a program that leaves them out, or rounds other values in their place, can miss the bound.
Values may be sent and summed in bfloat16 or wider, within the bound.
No kernel may reach another device: no remote copies, remote signals or barrier semaphores. Data moves between devices by JAX's collectives and lax.ppermute only.
A program may use at most 128 MiB of HBM per device.

```python
import math
import jax
import jax.numpy as jnp
from jax import lax

D = 512
H = 8
BS = 128
NB = 2
LOC = 3
EXP = 3
W = 2
CAPL = 1
KB = 7
GB = 64
NBLK = 1024
NODES = 131072
N_GROUP = 16
N_DOM = 32


def draw_queries(key, part):
    key = jax.random.fold_in(key, 11)
    return jnp.clip(jax.random.normal(key, (NODES, D), jnp.float32), -6.0, 6.0).astype(jnp.bfloat16)


def draw_keys(key, part):
    key = jax.random.fold_in(key, 13)
    return jnp.clip(jax.random.normal(key, (NODES, D), jnp.float32), -6.0, 6.0).astype(jnp.bfloat16)


def shuffled(subkey):
    return jax.random.permutation(subkey, NB)


def draw_local_list(key, part):
    key = jax.random.fold_in(key, 21)
    subkeys = jax.random.split(key, 2)
    doms = GB // NB
    devices = NBLK // NB
    reach = 2 * W
    dom_pos = jnp.arange(devices, dtype=jnp.int32) % doms
    offsets = jnp.concatenate([jnp.arange(-W, 0, dtype=jnp.int32), jnp.arange(1, W + 1, dtype=jnp.int32)])
    orders = jax.vmap(shuffled)(jax.random.split(subkeys[0], devices * reach)).reshape(devices, reach, NB)
    orders = orders[:, :, :CAPL].astype(jnp.int32)
    holder = dom_pos[:, None] + offsets[None, :]
    inside = (holder >= 0) & (holder < doms)
    remote_pos = holder[:, :, None] * NB + orders
    own_pos = dom_pos[:, None] * NB + jnp.arange(NB, dtype=jnp.int32)[None, :]
    fallback = own_pos[:, jnp.arange(reach * CAPL) % NB].reshape(devices, reach, CAPL)
    remote = jnp.where(inside[:, :, None], remote_pos, fallback).reshape(devices, reach * CAPL)
    candidates = jnp.concatenate([own_pos, remote], axis=1)
    picks = jax.random.randint(subkeys[1], (devices, NB * LOC), 0, NB + reach * CAPL)
    entries = jnp.take_along_axis(candidates, picks, axis=1)
    forced_index = jnp.arange(reach * CAPL)
    forced = forced_index % NB * LOC + forced_index // NB
    entries = entries.at[:, forced].set(remote)
    return entries.reshape(NBLK, LOC).astype(jnp.int32)


def draw_far_list(key, part):
    key = jax.random.fold_in(key, 31)
    subkeys = jax.random.split(key, 2)
    doms = GB // NB
    groups = NBLK // GB
    selected = jax.random.randint(subkeys[0], (doms, groups, groups), 0, NB)
    moved = jax.random.randint(subkeys[1], (doms, groups, NB * EXP), 1, groups)
    source = jnp.arange(groups, dtype=jnp.int32)[None, :, None]
    target = (source + moved) % groups
    slot_pick = jnp.take_along_axis(selected, target, axis=2)
    return (target * NB + slot_pick).reshape(doms, groups * NB, EXP).astype(jnp.int32)


def level_of(own_key, dims, shards, least, largest):
    gain, own = 1.0, jax.random.fold_in(own_key, 6)
    for dim, parts in shards:
        heights = jnp.exp(jax.random.uniform(jax.random.fold_in(own, dim), (parts,), jnp.float32, least / len(shards), largest / len(shards)))
        gain = gain * jnp.repeat(heights, dims[dim] // parts).reshape([-1 if axis == dim else 1 for axis in range(len(dims))])
    return gain


def noise(own_key, shape, spread, limit, cuts=(), kind=jnp.bfloat16):
    loudness = level_of(own_key, shape, cuts, -0.22, 0.18) if cuts else 1.0
    array = jax.random.normal(own_key, shape, jnp.float32) * spread * loudness
    return jnp.minimum(jnp.maximum(array, -limit), limit).astype(kind)


def setup_inputs(seed: int = 0) -> dict:
    splits = jax.random.split(jax.random.key(seed), 7)
    return {
        "queries": draw_queries(jax.random.fold_in(splits[6], 71), 0),
        "keys": draw_keys(jax.random.fold_in(splits[6], 71), 0),
        "values": noise(splits[2], (NODES, D), 1.0, 6.0, ((0, 512),)),
        "cotangent": noise(splits[3], (NODES, D), 1.0, 6.0, ((0, 512),)),
        "local_list": draw_local_list(jax.random.fold_in(splits[6], 71), 0),
        "far_list": draw_far_list(jax.random.fold_in(splits[6], 71), 0),
    }


def attend_block(query_blk, grad_blk, key_set, value_set):
    head_size = D // H
    score_scale = 1.0 / math.sqrt(head_size)
    query_heads = query_blk.astype(jnp.float32).reshape(BS, H, head_size)
    grad_heads = grad_blk.astype(jnp.float32).reshape(BS, H, head_size)
    key_heads = key_set.astype(jnp.float32).reshape(-1, H, head_size)
    value_heads = value_set.astype(jnp.float32).reshape(-1, H, head_size)
    scores = jnp.einsum('ihe,nhe->hin', query_heads, key_heads) * score_scale
    highest = lax.optimization_barrier(jnp.max(scores, axis=-1, keepdims=True))
    raised = jnp.exp(scores - highest)
    attention = raised / lax.optimization_barrier(jnp.sum(raised, axis=-1, keepdims=True))
    attention_low = attention.astype(jnp.bfloat16).astype(jnp.float32)
    mixture = jnp.einsum('hin,nhe->ihe', attention_low, value_heads)
    carried = lax.optimization_barrier(jnp.sum(grad_heads * mixture, axis=-1))
    grad_attention = jnp.einsum('ihe,nhe->hin', grad_heads, value_heads)
    grad_scores = (attention * (grad_attention - carried.T[:, :, None]) * score_scale).astype(jnp.bfloat16)
    grad_scores = grad_scores.astype(jnp.float32)
    grad_query = jnp.einsum('hin,nhe->ihe', grad_scores, key_heads)
    grad_key = jnp.einsum('hin,ihe->nhe', grad_scores, query_heads)
    grad_value = jnp.einsum('hin,ihe->nhe', attention_low, grad_heads)
    return (mixture.reshape(BS, D).astype(jnp.bfloat16), grad_query.reshape(BS, D).astype(jnp.bfloat16), grad_key.reshape(-1, BS, D), grad_value.reshape(-1, BS, D))

def reference(queries, keys, values, cotangent, local_list, far_list):
    devices = N_GROUP * N_DOM
    blocks = devices * NB
    cluster = N_DOM * NB
    block_ids = jnp.arange(blocks, dtype=jnp.int32)
    group_of = block_ids // cluster
    dom_of = block_ids // NB % N_DOM
    slot_of = block_ids % NB
    local_ids = group_of[:, None] * cluster + local_list
    far_values = far_list[dom_of, group_of * NB + slot_of]
    far_ids = far_values // NB * cluster + dom_of[:, None] * NB + far_values % NB
    listed = jnp.concatenate([block_ids[:, None], local_ids, far_ids], axis=1).astype(jnp.int32)
    listed_dev = listed.reshape(devices, NB * KB)
    query_blocks = queries.reshape(devices, NB, BS, D)
    grad_blocks = cotangent.reshape(devices, NB, BS, D)
    key_blocks = keys.reshape(blocks, BS, D)
    value_blocks = values.reshape(blocks, BS, D)
    entries = NB * KB
    earlier = jnp.arange(entries)[:, None] > jnp.arange(entries)[None, :]

    def per_device(totals, inputs):
        key_total, value_total = totals
        query_dev, grad_dev, listed_ids = inputs
        key_sets = key_blocks[listed_ids].reshape(NB, KB * BS, D)
        value_sets = value_blocks[listed_ids].reshape(NB, KB * BS, D)
        mixture, grad_query, grad_key, grad_value = jax.vmap(attend_block)(query_dev, grad_dev, key_sets, value_sets)
        matches = listed_ids[:, None] == listed_ids[None, :]
        leading = jnp.logical_not(jnp.any(matches & earlier, axis=1))
        combine = matches.astype(jnp.float32)
        key_part = jnp.einsum('ef,frd->erd', combine, grad_key.reshape(entries, BS, D)).astype(jnp.bfloat16)
        value_part = jnp.einsum('ef,frd->erd', combine, grad_value.reshape(entries, BS, D)).astype(jnp.bfloat16)
        weight = leading.astype(jnp.float32)[:, None, None]
        key_total = key_total.at[listed_ids].add(key_part.astype(jnp.float32) * weight)
        value_total = value_total.at[listed_ids].add(value_part.astype(jnp.float32) * weight)
        return ((key_total, value_total), (mixture, grad_query))
    empty_acc = jnp.zeros((blocks, BS, D), jnp.float32)
    totals, stacked = lax.scan(per_device, (empty_acc, empty_acc), (query_blocks, grad_blocks, listed_dev))
    key_total, value_total = totals
    mixture, grad_query = stacked
    return (mixture.reshape(NODES, D), grad_query.reshape(NODES, D), key_total.astype(jnp.bfloat16).reshape(NODES, D), value_total.astype(jnp.bfloat16).reshape(NODES, D))
```

```python
import functools
import math

import jax
import jax.numpy as jnp
from jax import lax
from jax.experimental import pallas as pl
from jax.experimental.pallas import tpu as pltpu
from jax.sharding import PartitionSpec as P

D = 512
BS = 128
NB = 2
LOC = 3
EXP = 3
W = 2
KB = 1 + LOC + EXP
ENTRIES = NB * KB
ROWS = KB * BS
FAR = NB * EXP
NEAR = NB + 2 * W
PAIRS = D // 128
BF = jnp.bfloat16
F32 = jnp.float32
OFFSETS = (-2, -1, 1, 2)

ANY = pl.BlockSpec(memory_space=pl.ANY)
VMEM = pl.BlockSpec(memory_space=pltpu.VMEM)
SMEM = pl.BlockSpec(memory_space=pltpu.SMEM)

SIBLING, FLOW_A, FLOW_B, PICKED = 0, 0, 4, 8


def ring_step(array):
    size = lax.axis_size("group")
    return lax.ppermute(array, "group", [(g, (g + (2 if g % 2 == 0 else -2)) % size) for g in range(size)])


def swap_cores(array):
    size = lax.axis_size("group")
    return lax.ppermute(array, "group", [(g, g ^ 1) for g in range(size)])


def shifted(array, by):
    size = lax.axis_size("dom")
    return lax.ppermute(array, "dom", [(i, i + by) for i in range(size) if 0 <= i + by < size])


def place_of(cluster, chip, core, chips):
    other_chip, other_core = cluster // 2, cluster % 2
    distance = jnp.where(core == 0, chip - other_chip, other_chip - chip) % chips
    same = other_core == core
    half = chips // 2
    here = jnp.where(same, FLOW_A + distance, FLOW_B + distance)
    held = jnp.where(same, distance <= half, distance < half)
    return jnp.where(distance == 0, SIBLING, jnp.where(held, here, PICKED))


def first_of(values):
    order = jnp.arange(values.shape[0], dtype=jnp.int32)
    same = values[:, None] == values[None, :]
    return jnp.min(jnp.where(same, order[None, :], values.shape[0]), axis=1)


def slot_in(values, wanted):
    order = jnp.arange(values.shape[0], dtype=jnp.int32)
    hit = values[None, :] == wanted[:, None]
    found = jnp.min(jnp.where(hit, order[None, :], values.shape[0]), axis=1)
    return jnp.where(found == values.shape[0], -1, found).astype(jnp.int32)


def pick_kernel(table, *refs):
    places, out, sem = refs[:8], refs[8], refs[9]
    copies = []
    for t in range(FAR):
        for code, place in enumerate(places):

            @pl.when(table[0, t] == code)
            def _():
                rows = pl.ds(pl.multiple_of(table[1, t] * BS, BS), BS)
                pltpu.make_async_copy(place.at[:, rows, :], out.at[t], sem.at[t]).start()

    for t in range(FAR):

        @pl.when(table[0, t] < 8)
        def _():
            pltpu.make_async_copy(places[0].at[:, pl.ds(0, BS), :], out.at[t], sem.at[t]).wait()


def pick(table, places):
    return pl.pallas_call(
        pick_kernel,
        out_shape=jax.ShapeDtypeStruct((FAR, 2, BS, D), BF),
        in_specs=[SMEM] + [ANY] * 8,
        out_specs=ANY,
        scratch_shapes=[pltpu.SemaphoreType.DMA((FAR,))],
        cost_estimate=pl.CostEstimate(flops=0, bytes_accessed=6 * 2**20, transcendentals=0),
    )(table, *places)


def attend_pair(step, table, q_ref, g_ref, listed, att_ref, gq_ref, totals):
    low = lax.broadcasted_iota(jnp.int32, (BS, 128), 1) < 64
    last = (((1,), (1,)), ((), ()))
    first = (((0,), (0,)), ((), ()))
    s = step // PAIRS
    p = step % PAIRS
    cols = pl.ds(pl.multiple_of(p * 128, 128), 128)
    query = q_ref[s, :, cols]
    grad = g_ref[s, :, cols]
    zero = jnp.zeros_like(query)
    query2 = jnp.concatenate([jnp.where(low, query, zero), jnp.where(low, zero, query)], axis=0)
    grad2 = jnp.concatenate([jnp.where(low, grad, zero), jnp.where(low, zero, grad)], axis=0)
    keys = listed[s, 0, :, cols]
    values = listed[s, 1, :, cols]

    def own_heads(both):
        return jnp.concatenate([both[:64, :128], both[64:, 128:]], axis=0)

    scores = lax.dot_general(keys, query2, last, preferred_element_type=F32)
    highest = jnp.max(scores, axis=0, keepdims=True)
    raised = jnp.exp2((scores - highest) * (0.125 * math.log2(math.e)))
    weights = raised * (1.0 / jnp.sum(raised, axis=0, keepdims=True))
    weights_low = weights.astype(BF)
    mixture = own_heads(lax.dot_general(values, weights_low, first, preferred_element_type=F32))
    att_ref[s, :, cols] = mixture.T.astype(BF)
    product = mixture * grad.astype(F32).T
    carried = jnp.concatenate(
        [jnp.sum(product[:64], axis=0, keepdims=True), jnp.sum(product[64:], axis=0, keepdims=True)], axis=1
    )
    grad_weights = lax.dot_general(values, grad2, last, preferred_element_type=F32)
    grad_scores = ((weights * (grad_weights - carried)) * 0.125).astype(BF)
    grad_query = own_heads(lax.dot_general(keys, grad_scores, first, preferred_element_type=F32))
    gq_ref[s, :, cols] = grad_query.T.astype(BF)
    grad_key = jnp.dot(grad_scores, query2, preferred_element_type=F32)
    grad_value = jnp.dot(weights_low, grad2, preferred_element_type=F32)
    for j in range(KB):
        slot = table[2, s * KB + j]
        leads = table[3, s * KB + j]
        rows = slice(j * BS, (j + 1) * BS)

        @pl.when(leads == 1)
        def _():
            totals[slot, 0, :, cols] = grad_key[rows]
            totals[slot, 1, :, cols] = grad_value[rows]

        @pl.when(leads == 0)
        def _():
            totals[slot, 0, :, cols] += grad_key[rows]
            totals[slot, 1, :, cols] += grad_value[rows]


def attend_kernel(table, q_ref, g_ref, *refs):
    own, near, places, picked = refs[0], refs[1:5], refs[5:13], refs[13]
    att_ref, gq_ref, near_out, far_out, listed, totals, sem = refs[14:]

    def bring(source, s, j):
        pltpu.make_async_copy(source, listed.at[s, :, pl.ds(j * BS, BS), :], sem.at[s]).start()

    for s in range(NB):
        bring(own.at[:, pl.ds(s * BS, BS), :], s, 0)
        for j in range(1, KB):
            code, place = table[0, s * KB + j], table[1, s * KB + j]
            rows = pl.ds(pl.multiple_of(place * BS, BS), BS)
            if j <= LOC:

                @pl.when(code == 0)
                def _():
                    bring(own.at[:, rows, :], s, j)

                for t in range(2 * W):

                    @pl.when(code == 1 + t)
                    def _():
                        bring(near[t], s, j)

            else:
                for t in range(8):

                    @pl.when(code == t)
                    def _():
                        bring(places[t].at[:, rows, :], s, j)

                @pl.when(code == 8)
                def _():
                    bring(picked.at[s * EXP + j - 1 - LOC], s, j)

    for s in range(NB):
        pltpu.make_async_copy(listed.at[s], listed.at[s], sem.at[s]).wait()

    def body(step, carry):
        attend_pair(step, table, q_ref, g_ref, listed, att_ref, gq_ref, totals)
        return carry

    lax.fori_loop(0, NB * PAIRS, body, 0)
    near_out[...] = totals[:NEAR].astype(BF)
    far_out[...] = totals[NEAR:].astype(BF)


def attend(table, queries, cotangent, own, near, places, picked):
    return pl.pallas_call(
        attend_kernel,
        out_shape=(
            jax.ShapeDtypeStruct((NB, BS, D), BF),
            jax.ShapeDtypeStruct((NB, BS, D), BF),
            jax.ShapeDtypeStruct((NEAR, 2, BS, D), BF),
            jax.ShapeDtypeStruct((FAR, 2, BS, D), BF),
        ),
        in_specs=[SMEM, VMEM, VMEM] + [ANY] * 14,
        out_specs=(VMEM, VMEM, VMEM, VMEM),
        scratch_shapes=[
            pltpu.VMEM((NB, 2, ROWS, D), BF),
            pltpu.VMEM((NEAR + FAR, 2, BS, D), F32),
            pltpu.SemaphoreType.DMA((NB,)),
        ],
        compiler_params=pltpu.CompilerParams(vmem_limit_bytes=40 * 2**20),
        cost_estimate=pl.CostEstimate(
            flops=12 * NB * BS * ROWS * D, bytes_accessed=12 * 2**20, transcendentals=NB * 8 * BS * ROWS
        ),
    )(table, queries, cotangent, own, *near, *places, picked)


def spread_kernel(count, table, mine, theirs, *outs):
    for n in range(count):
        out = outs[n]
        for s in range(NB):
            a, b = table[0, n * NB + s], table[1, n * NB + s]

            @pl.when((a < 0) & (b < 0))
            def _():
                out[s] = jnp.zeros((2, BS, D), BF)

            @pl.when((a >= 0) & (b < 0))
            def _():
                out[s] = mine[a]

            @pl.when((a < 0) & (b >= 0))
            def _():
                out[s] = theirs[b]

            @pl.when((a >= 0) & (b >= 0))
            def _():
                out[s] = (mine[a].astype(F32) + theirs[b].astype(F32)).astype(BF)


def spread(table, mine, theirs):
    count = table.shape[1] // NB
    return pl.pallas_call(
        functools.partial(spread_kernel, count),
        out_shape=tuple(jax.ShapeDtypeStruct((NB, 2, BS, D), BF) for _ in range(count)),
        in_specs=[SMEM, VMEM, VMEM],
        out_specs=(VMEM,) * count,
        compiler_params=pltpu.CompilerParams(vmem_limit_bytes=24 * 2**20),
        cost_estimate=pl.CostEstimate(flops=0, bytes_accessed=(3 + count) * 2**19, transcendentals=0),
    )(table, mine, theirs)


def close_kernel(table, near, theirs, from_a, from_b, *refs):
    returned, (gk_ref, gv_ref) = refs[:4], refs[4:]
    for s in range(NB):
        for half, out in enumerate((gk_ref, gv_ref)):
            total = near[s, half].astype(F32)
            for t in range(2 * W):
                total = total + jnp.where(table[t] == s, returned[t][half].astype(F32), 0.0)
            total = total + from_a[s, half].astype(F32) + from_b[s, half].astype(F32)
            b = table[4 + s]
            direct = theirs[jnp.maximum(b, 0), half].astype(F32)
            total = total + jnp.where(b >= 0, direct, 0.0)
            out[pl.ds(s * BS, BS), :] = total.astype(BF)


def close(table, near, theirs, from_a, from_b, returned):
    return pl.pallas_call(
        close_kernel,
        out_shape=(jax.ShapeDtypeStruct((NB * BS, D), BF),) * 2,
        in_specs=[SMEM] + [VMEM] * 8,
        out_specs=(VMEM, VMEM),
        compiler_params=pltpu.CompilerParams(vmem_limit_bytes=24 * 2**20),
        cost_estimate=pl.CostEstimate(flops=2**22, bytes_accessed=6 * 2**20, transcendentals=0),
    )(table, near, theirs, from_a, from_b, *returned)


def on_device(queries, keys, values, cotangent, local_list, far_list):
    groups = lax.axis_size("group")
    doms = lax.axis_size("dom")
    chips = groups // 2
    dom = lax.axis_index("dom").astype(jnp.int32)
    group = lax.axis_index("group").astype(jnp.int32)
    chip, core = group // 2, group % 2
    i32 = jnp.int32

    own = jnp.stack([keys, values])
    flow_a = [ring_step(own)]
    sibling = swap_cores(own)
    flow_b = [ring_step(sibling)]
    for _ in range(2):
        flow_a.append(ring_step(flow_a[-1]))
        flow_b.append(ring_step(flow_b[-1]))
    flow_a.append(ring_step(flow_a[-1]))

    padded = jnp.pad(local_list, ((W * NB, W * NB), (0, 0)), constant_values=-1)
    around = lax.dynamic_slice_in_dim(padded, dom * NB, (2 * W + 1) * NB, 0).reshape(2 * W + 1, NB * LOC)
    given = jnp.max(jnp.where(around // NB == dom, around % NB, 0), axis=1).astype(i32)
    blocks = own.reshape(2, NB, BS, D)
    near = []
    for offset in OFFSETS:
        piece = lax.dynamic_index_in_dim(blocks, given[W + offset], 1, keepdims=False)
        near.append(shifted(piece, offset))
    local = around[W].reshape(NB, LOC)
    holder = local // NB - dom
    near_code = jnp.where(holder == 0, 0, jnp.where(holder > 0, 3 - holder, 2 - holder))
    near_key = jnp.where(holder == 0, local % NB, NB - 1 + near_code)

    far_rows = far_list[0].reshape(groups, FAR)
    mine = lax.dynamic_index_in_dim(far_rows, group, 0, keepdims=False)
    theirs = lax.dynamic_index_in_dim(far_rows, group ^ 1, 0, keepdims=False)
    far_code = place_of(mine // NB, chip, core, chips)
    needed = place_of(theirs // NB, chip, 1 - core, chips) == PICKED
    sent = jnp.where(needed, place_of(theirs // NB, chip, core, chips), PICKED)
    picked = swap_cores(pick(jnp.stack([sent, theirs % NB]).astype(i32), [sibling] + flow_a + flow_b))

    self_code = jnp.zeros((NB, 1), i32)
    self_key = jnp.arange(NB, dtype=i32)[:, None]
    codes = jnp.concatenate([self_code, near_code, far_code.reshape(NB, EXP)], axis=1).reshape(-1)
    slots = jnp.concatenate([self_key, local % NB, (mine % NB).reshape(NB, EXP)], axis=1).reshape(-1)
    far_key = (NEAR + first_of(mine)).reshape(NB, EXP)
    targets = jnp.concatenate([self_key, near_key, far_key], axis=1).reshape(-1)
    leads = first_of(targets) == jnp.arange(ENTRIES, dtype=i32)
    table = jnp.stack([codes, slots, targets, leads.astype(i32)]).astype(i32)
    attended, grad_queries, near_terms, far_terms = attend(
        table,
        queries.reshape(NB, BS, D),
        cotangent.reshape(NB, BS, D),
        own,
        near,
        [sibling] + flow_a + flow_b,
        picked,
    )

    sibling_terms = swap_cores(far_terms)
    steps = [(4, 0), (3, 1), (3, 0), (2, 1), (2, 0), (1, 1), (1, 0)]
    direction = 1 - 2 * core
    wanted = []
    for distance, side in steps:
        cluster = ((chip + direction * distance) % chips) * 2 + jnp.where(side == 0, core, 1 - core)
        wanted += [cluster * NB, cluster * NB + 1]
    wanted += [group * NB, group * NB + 1]
    wanted = jnp.stack(wanted).astype(i32)
    hits = jnp.stack([slot_in(mine, wanted), slot_in(theirs, wanted)])
    start_a, start_b = spread(hits[:, : 2 * NB], far_terms, sibling_terms)
    a3, b2, a2, b1, a1 = spread(hits[:, 2 * NB : 7 * NB], far_terms, sibling_terms)

    def joined(x, y):
        return (x.astype(F32) + y.astype(F32)).astype(BF)

    back_a = ring_step(start_a)
    back_b = ring_step(start_b)
    back_a = ring_step(joined(back_a, a3))
    back_b = ring_step(joined(back_b, b2))
    back_a = ring_step(joined(back_a, a2))
    back_b = ring_step(joined(back_b, b1))
    back_a = ring_step(joined(back_a, a1))
    back_b = swap_cores(back_b)

    returned = [shifted(near_terms[NB + t], -offset) for t, offset in enumerate(OFFSETS)]
    back_slots = jnp.stack([given[W + offset] for offset in OFFSETS])
    last = jnp.concatenate([back_slots, hits[1, 7 * NB :]]).astype(i32)
    grad_keys, grad_values = close(last, near_terms[:NB], sibling_terms, back_a, back_b, returned)
    return (attended.reshape(NB * BS, D), grad_queries.reshape(NB * BS, D), grad_keys, grad_values)


def solution(mesh):
    rows = P(("group", "dom"), None)
    return jax.shard_map(
        on_device,
        mesh=mesh,
        in_specs=(rows, rows, rows, rows, P("group", None), P("dom", None, None)),
        out_specs=(rows, rows, rows, rows),
        check_vma=False,
    )
```

```python
import functools
import math

import jax
import jax.numpy as jnp
from jax import lax
from jax.experimental import pallas as pl
from jax.experimental.pallas import tpu as pltpu
from jax.sharding import PartitionSpec as P

D = 512
BS = 128
NB = 2
LOC = 3
EXP = 3
W = 2
KB = 1 + LOC + EXP
ENTRIES = NB * KB
ROWS = KB * BS
FAR = NB * EXP
NEAR = NB + 2 * W
PAIRS = D // 128
BF = jnp.bfloat16
F32 = jnp.float32
OFFSETS = (-2, -1, 1, 2)

ANY = pl.BlockSpec(memory_space=pl.ANY)
VMEM = pl.BlockSpec(memory_space=pltpu.VMEM)
SMEM = pl.BlockSpec(memory_space=pltpu.SMEM)

SIBLING, FLOW_A, FLOW_B, PICKED = 0, 0, 4, 8


def ring_step(array):
    size = lax.axis_size("group")
    return lax.ppermute(array, "group", [(g, (g + (2 if g % 2 == 0 else -2)) % size) for g in range(size)])


def swap_cores(array):
    size = lax.axis_size("group")
    return lax.ppermute(array, "group", [(g, g ^ 1) for g in range(size)])


def shifted(array, by):
    size = lax.axis_size("dom")
    return lax.ppermute(array, "dom", [(i, i + by) for i in range(size) if 0 <= i + by < size])


def place_of(cluster, chip, core, chips):
    other_chip, other_core = cluster // 2, cluster % 2
    distance = jnp.where(core == 0, chip - other_chip, other_chip - chip) % chips
    same = other_core == core
    half = chips // 2
    here = jnp.where(same, FLOW_A + distance, FLOW_B + distance)
    held = jnp.where(same, distance <= half, distance < half)
    return jnp.where(distance == 0, SIBLING, jnp.where(held, here, PICKED))


def first_of(values):
    order = jnp.arange(values.shape[0], dtype=jnp.int32)
    same = values[:, None] == values[None, :]
    return jnp.min(jnp.where(same, order[None, :], values.shape[0]), axis=1)


def slot_in(values, wanted):
    order = jnp.arange(values.shape[0], dtype=jnp.int32)
    hit = values[None, :] == wanted[:, None]
    found = jnp.min(jnp.where(hit, order[None, :], values.shape[0]), axis=1)
    return jnp.where(found == values.shape[0], -1, found).astype(jnp.int32)


def pick_kernel(table, *refs):
    places, out, sem = refs[:8], refs[8], refs[9]
    copies = []
    for t in range(FAR):
        for code, place in enumerate(places):

            @pl.when(table[0, t] == code)
            def _():
                rows = pl.ds(pl.multiple_of(table[1, t] * BS, BS), BS)
                pltpu.make_async_copy(place.at[:, rows, :], out.at[t], sem.at[t]).start()

    for t in range(FAR):

        @pl.when(table[0, t] < 8)
        def _():
            pltpu.make_async_copy(places[0].at[:, pl.ds(0, BS), :], out.at[t], sem.at[t]).wait()


def pick(table, places):
    return pl.pallas_call(
        pick_kernel,
        out_shape=jax.ShapeDtypeStruct((FAR, 2, BS, D), BF),
        in_specs=[SMEM] + [ANY] * 8,
        out_specs=VMEM,
        scratch_shapes=[pltpu.SemaphoreType.DMA((FAR,))],
        compiler_params=pltpu.CompilerParams(vmem_limit_bytes=4 * 2**20),
        cost_estimate=pl.CostEstimate(flops=0, bytes_accessed=6 * 2**20, transcendentals=0),
    )(table, *places)


def attend_pair(step, table, q_ref, g_ref, listed, att_ref, gq_ref, totals):
    low = lax.broadcasted_iota(jnp.int32, (BS, 128), 1) < 64
    last = (((1,), (1,)), ((), ()))
    first = (((0,), (0,)), ((), ()))
    s = step // PAIRS
    p = step % PAIRS
    cols = pl.ds(pl.multiple_of(p * 128, 128), 128)
    query = q_ref[s, :, cols]
    grad = g_ref[s, :, cols]
    zero = jnp.zeros_like(query)
    query2 = jnp.concatenate([jnp.where(low, query, zero), jnp.where(low, zero, query)], axis=0)
    grad2 = jnp.concatenate([jnp.where(low, grad, zero), jnp.where(low, zero, grad)], axis=0)
    keys = listed[s, 0, :, cols]
    values = listed[s, 1, :, cols]

    def own_heads(both):
        return jnp.concatenate([both[:64, :128], both[64:, 128:]], axis=0)

    scores = lax.dot_general(keys, query2, last, preferred_element_type=F32)
    highest = jnp.max(scores, axis=0, keepdims=True)
    raised = jnp.exp2((scores - highest) * (0.125 * math.log2(math.e)))
    weights = raised * (1.0 / jnp.sum(raised, axis=0, keepdims=True))
    weights_low = weights.astype(BF)
    mixture = own_heads(lax.dot_general(values, weights_low, first, preferred_element_type=F32))
    att_ref[s, :, cols] = mixture.T.astype(BF)
    product = mixture * grad.astype(F32).T
    carried = jnp.concatenate(
        [jnp.sum(product[:64], axis=0, keepdims=True), jnp.sum(product[64:], axis=0, keepdims=True)], axis=1
    )
    grad_weights = lax.dot_general(values, grad2, last, preferred_element_type=F32)
    grad_scores = ((weights * (grad_weights - carried)) * 0.125).astype(BF)
    grad_query = own_heads(lax.dot_general(keys, grad_scores, first, preferred_element_type=F32))
    gq_ref[s, :, cols] = grad_query.T.astype(BF)
    grad_key = jnp.dot(grad_scores, query2, preferred_element_type=F32)
    grad_value = jnp.dot(weights_low, grad2, preferred_element_type=F32)
    for j in range(KB):
        slot = table[2, s * KB + j]
        leads = table[3, s * KB + j]
        rows = slice(j * BS, (j + 1) * BS)

        @pl.when(leads == 1)
        def _():
            totals[slot, 0, :, cols] = grad_key[rows]
            totals[slot, 1, :, cols] = grad_value[rows]

        @pl.when(leads == 0)
        def _():
            totals[slot, 0, :, cols] += grad_key[rows]
            totals[slot, 1, :, cols] += grad_value[rows]


def attend_kernel(table, q_ref, g_ref, *refs):
    own, near, places, picked = refs[0], refs[1:5], refs[5:13], refs[13]
    att_ref, gq_ref, near_out, far_out, listed, totals, sem = refs[14:]

    def bring(source, s, j):
        pltpu.make_async_copy(source, listed.at[s, :, pl.ds(j * BS, BS), :], sem.at[s]).start()

    for s in range(NB):
        bring(own.at[:, pl.ds(s * BS, BS), :], s, 0)
        for j in range(1, KB):
            code, place = table[0, s * KB + j], table[1, s * KB + j]
            rows = pl.ds(pl.multiple_of(place * BS, BS), BS)
            if j <= LOC:

                @pl.when(code == 0)
                def _():
                    bring(own.at[:, rows, :], s, j)

                for t in range(2 * W):

                    @pl.when(code == 1 + t)
                    def _():
                        bring(near[t], s, j)

            else:
                for t in range(8):

                    @pl.when(code == t)
                    def _():
                        bring(places[t].at[:, rows, :], s, j)

                @pl.when(code == 8)
                def _():
                    bring(picked.at[s * EXP + j - 1 - LOC], s, j)

    for s in range(NB):
        pltpu.make_async_copy(listed.at[s], listed.at[s], sem.at[s]).wait()

    def body(step, carry):
        attend_pair(step, table, q_ref, g_ref, listed, att_ref, gq_ref, totals)
        return carry

    lax.fori_loop(0, NB * PAIRS, body, 0)
    near_out[...] = totals[:NEAR].astype(BF)
    far_out[...] = totals[NEAR:].astype(BF)


def attend(table, queries, cotangent, own, near, places, picked):
    return pl.pallas_call(
        attend_kernel,
        out_shape=(
            jax.ShapeDtypeStruct((NB, BS, D), BF),
            jax.ShapeDtypeStruct((NB, BS, D), BF),
            jax.ShapeDtypeStruct((NEAR, 2, BS, D), BF),
            jax.ShapeDtypeStruct((FAR, 2, BS, D), BF),
        ),
        in_specs=[SMEM, VMEM, VMEM] + [ANY] * 14,
        out_specs=(VMEM, VMEM, VMEM, VMEM),
        scratch_shapes=[
            pltpu.VMEM((NB, 2, ROWS, D), BF),
            pltpu.VMEM((NEAR + FAR, 2, BS, D), F32),
            pltpu.SemaphoreType.DMA((NB,)),
        ],
        compiler_params=pltpu.CompilerParams(vmem_limit_bytes=32 * 2**20),
        cost_estimate=pl.CostEstimate(
            flops=12 * NB * BS * ROWS * D, bytes_accessed=12 * 2**20, transcendentals=NB * 8 * BS * ROWS
        ),
    )(table, queries, cotangent, own, *near, *places, picked)


def spread_kernel(count, table, mine, theirs, *outs):
    for n in range(count):
        out = outs[n]
        for s in range(NB):
            a, b = table[0, n * NB + s], table[1, n * NB + s]

            @pl.when((a < 0) & (b < 0))
            def _():
                out[s] = jnp.zeros((2, BS, D), BF)

            @pl.when((a >= 0) & (b < 0))
            def _():
                out[s] = mine[a]

            @pl.when((a < 0) & (b >= 0))
            def _():
                out[s] = theirs[b]

            @pl.when((a >= 0) & (b >= 0))
            def _():
                out[s] = (mine[a].astype(F32) + theirs[b].astype(F32)).astype(BF)


def spread(table, mine, theirs):
    count = table.shape[1] // NB
    return pl.pallas_call(
        functools.partial(spread_kernel, count),
        out_shape=tuple(jax.ShapeDtypeStruct((NB, 2, BS, D), BF) for _ in range(count)),
        in_specs=[SMEM, VMEM, VMEM],
        out_specs=(VMEM,) * count,
        compiler_params=pltpu.CompilerParams(vmem_limit_bytes=12 * 2**20),
        cost_estimate=pl.CostEstimate(flops=0, bytes_accessed=(3 + count) * 2**19, transcendentals=0),
    )(table, mine, theirs)


def close_kernel(table, near, theirs, from_a, from_b, *refs):
    returned, (gk_ref, gv_ref) = refs[:4], refs[4:]
    for s in range(NB):
        for half, out in enumerate((gk_ref, gv_ref)):
            total = near[s, half].astype(F32)
            for t in range(2 * W):
                total = total + jnp.where(table[t] == s, returned[t][half].astype(F32), 0.0)
            total = total + from_a[s, half].astype(F32) + from_b[s, half].astype(F32)
            b = table[4 + s]
            direct = theirs[jnp.maximum(b, 0), half].astype(F32)
            total = total + jnp.where(b >= 0, direct, 0.0)
            out[pl.ds(s * BS, BS), :] = total.astype(BF)


def close(table, near, theirs, from_a, from_b, returned):
    return pl.pallas_call(
        close_kernel,
        out_shape=(jax.ShapeDtypeStruct((NB * BS, D), BF),) * 2,
        in_specs=[SMEM] + [VMEM] * 8,
        out_specs=(VMEM, VMEM),
        compiler_params=pltpu.CompilerParams(vmem_limit_bytes=12 * 2**20),
        cost_estimate=pl.CostEstimate(flops=2**22, bytes_accessed=6 * 2**20, transcendentals=0),
    )(table, near, theirs, from_a, from_b, *returned)


def on_device(queries, keys, values, cotangent, local_list, far_list):
    groups = lax.axis_size("group")
    doms = lax.axis_size("dom")
    chips = groups // 2
    dom = lax.axis_index("dom").astype(jnp.int32)
    group = lax.axis_index("group").astype(jnp.int32)
    chip, core = group // 2, group % 2
    i32 = jnp.int32

    own = jnp.stack([keys, values])
    flow_a = [ring_step(own)]
    sibling = swap_cores(own)
    flow_b = [ring_step(sibling)]

    padded = jnp.pad(local_list, ((W * NB, W * NB), (0, 0)), constant_values=-1)
    around = lax.dynamic_slice_in_dim(padded, dom * NB, (2 * W + 1) * NB, 0).reshape(2 * W + 1, NB * LOC)
    given = jnp.max(jnp.where(around // NB == dom, around % NB, 0), axis=1).astype(i32)
    blocks = own.reshape(2, NB, BS, D)
    near = []
    for offset in OFFSETS:
        piece = lax.dynamic_index_in_dim(blocks, given[W + offset], 1, keepdims=False)
        near.append(shifted(piece, offset))
    flow_a[0], near = lax.optimization_barrier((flow_a[0], near))
    for _ in range(2):
        flow_a.append(ring_step(flow_a[-1]))
        flow_b.append(ring_step(flow_b[-1]))
    flow_a.append(ring_step(flow_a[-1]))

    local = around[W].reshape(NB, LOC)
    holder = local // NB - dom
    near_code = jnp.where(holder == 0, 0, jnp.where(holder > 0, 3 - holder, 2 - holder))
    near_key = jnp.where(holder == 0, local % NB, NB - 1 + near_code)

    far_rows = far_list[0].reshape(groups, FAR)
    mine = lax.dynamic_index_in_dim(far_rows, group, 0, keepdims=False)
    theirs = lax.dynamic_index_in_dim(far_rows, group ^ 1, 0, keepdims=False)
    far_code = place_of(mine // NB, chip, core, chips)
    needed = place_of(theirs // NB, chip, 1 - core, chips) == PICKED
    sent = jnp.where(needed, place_of(theirs // NB, chip, core, chips), PICKED)
    picked = swap_cores(pick(jnp.stack([sent, theirs % NB]).astype(i32), [sibling] + flow_a + flow_b))

    self_code = jnp.zeros((NB, 1), i32)
    self_key = jnp.arange(NB, dtype=i32)[:, None]
    codes = jnp.concatenate([self_code, near_code, far_code.reshape(NB, EXP)], axis=1).reshape(-1)
    slots = jnp.concatenate([self_key, local % NB, (mine % NB).reshape(NB, EXP)], axis=1).reshape(-1)
    far_key = (NEAR + first_of(mine)).reshape(NB, EXP)
    targets = jnp.concatenate([self_key, near_key, far_key], axis=1).reshape(-1)
    leads = first_of(targets) == jnp.arange(ENTRIES, dtype=i32)
    table = jnp.stack([codes, slots, targets, leads.astype(i32)]).astype(i32)
    attended, grad_queries, near_terms, far_terms = attend(
        table,
        queries.reshape(NB, BS, D),
        cotangent.reshape(NB, BS, D),
        own,
        near,
        [sibling] + flow_a + flow_b,
        picked,
    )

    sibling_terms = swap_cores(far_terms)
    steps = [(4, 0), (3, 1), (3, 0), (2, 1), (2, 0), (1, 1), (1, 0)]
    direction = 1 - 2 * core
    wanted = []
    for distance, side in steps:
        cluster = ((chip + direction * distance) % chips) * 2 + jnp.where(side == 0, core, 1 - core)
        wanted += [cluster * NB, cluster * NB + 1]
    wanted += [group * NB, group * NB + 1]
    wanted = jnp.stack(wanted).astype(i32)
    hits = jnp.stack([slot_in(mine, wanted), slot_in(theirs, wanted)])
    start_a, start_b = spread(hits[:, : 2 * NB], far_terms, sibling_terms)
    a3, b2, a2, b1, a1 = spread(hits[:, 2 * NB : 7 * NB], far_terms, sibling_terms)

    def joined(x, y):
        return (x.astype(F32) + y.astype(F32)).astype(BF)

    returned = [shifted(near_terms[NB + t], -offset) for t, offset in enumerate(OFFSETS)]
    back_a = ring_step(start_a)
    back_b = ring_step(start_b)
    back_a, returned = lax.optimization_barrier((back_a, returned))
    back_a = ring_step(joined(back_a, a3))
    back_b = ring_step(joined(back_b, b2))
    back_a = ring_step(joined(back_a, a2))
    back_b = ring_step(joined(back_b, b1))
    back_a = ring_step(joined(back_a, a1))
    back_b = swap_cores(back_b)

    back_slots = jnp.stack([given[W + offset] for offset in OFFSETS])
    last = jnp.concatenate([back_slots, hits[1, 7 * NB :]]).astype(i32)
    grad_keys, grad_values = close(last, near_terms[:NB], sibling_terms, back_a, back_b, returned)
    return (attended.reshape(NB * BS, D), grad_queries.reshape(NB * BS, D), grad_keys, grad_values)


def solution(mesh):
    rows = P(("group", "dom"), None)
    return jax.shard_map(
        on_device,
        mesh=mesh,
        in_specs=(rows, rows, rows, rows, P("group", None), P("dom", None, None)),
        out_specs=(rows, rows, rows, rows),
        check_vma=False,
    )
```

```python
import functools
import math

import jax
import jax.numpy as jnp
from jax import lax
from jax.experimental import pallas as pl
from jax.experimental.pallas import tpu as pltpu
from jax.sharding import PartitionSpec as P

D = 512
BS = 128
NB = 2
LOC = 3
EXP = 3
W = 2
KB = 1 + LOC + EXP
ENTRIES = NB * KB
ROWS = KB * BS
FAR = NB * EXP
NEAR = NB + 2 * W
PAIRS = D // 128
BF = jnp.bfloat16
F32 = jnp.float32
OFFSETS = (-2, -1, 1, 2)

HBM = pl.BlockSpec(memory_space=pltpu.HBM)
VMEM = pl.BlockSpec(memory_space=pltpu.VMEM)
SMEM = pl.BlockSpec(memory_space=pltpu.SMEM)

SIBLING, FLOW_A, FLOW_B, PICKED = 0, 0, 4, 8


def ring_step(array):
    size = lax.axis_size("group")
    return lax.ppermute(array, "group", [(g, (g + (2 if g % 2 == 0 else -2)) % size) for g in range(size)])


def swap_cores(array):
    size = lax.axis_size("group")
    return lax.ppermute(array, "group", [(g, g ^ 1) for g in range(size)])


def shifted(array, by):
    size = lax.axis_size("dom")
    return lax.ppermute(array, "dom", [(i, i + by) for i in range(size) if 0 <= i + by < size])


def place_of(cluster, chip, core, chips):
    other_chip, other_core = cluster // 2, cluster % 2
    distance = jnp.where(core == 0, chip - other_chip, other_chip - chip) % chips
    same = other_core == core
    half = chips // 2
    here = jnp.where(same, FLOW_A + distance, FLOW_B + distance)
    held = jnp.where(same, distance <= half, distance < half)
    return jnp.where(distance == 0, SIBLING, jnp.where(held, here, PICKED))


def first_of(values):
    order = jnp.arange(values.shape[0], dtype=jnp.int32)
    same = values[:, None] == values[None, :]
    return jnp.min(jnp.where(same, order[None, :], values.shape[0]), axis=1)


def slot_in(values, wanted):
    order = jnp.arange(values.shape[0], dtype=jnp.int32)
    hit = values[None, :] == wanted[:, None]
    found = jnp.min(jnp.where(hit, order[None, :], values.shape[0]), axis=1)
    return jnp.where(found == values.shape[0], -1, found).astype(jnp.int32)


def pick_kernel(table, *refs):
    places, out, sem = refs[:8], refs[8], refs[9]
    copies = []
    for t in range(FAR):
        for code, place in enumerate(places):

            @pl.when(table[0, t] == code)
            def _():
                rows = pl.ds(pl.multiple_of(table[1, t] * BS, BS), BS)
                pltpu.make_async_copy(place.at[:, rows, :], out.at[t], sem.at[t]).start()

    for t in range(FAR):

        @pl.when(table[0, t] < 8)
        def _():
            pltpu.make_async_copy(places[0].at[:, pl.ds(0, BS), :], out.at[t], sem.at[t]).wait()


def pick(table, places):
    return pl.pallas_call(
        pick_kernel,
        out_shape=jax.ShapeDtypeStruct((FAR, 2, BS, D), BF),
        in_specs=[SMEM] + [HBM] * 8,
        out_specs=VMEM,
        scratch_shapes=[pltpu.SemaphoreType.DMA((FAR,))],
        compiler_params=pltpu.CompilerParams(vmem_limit_bytes=4 * 2**20),
        cost_estimate=pl.CostEstimate(flops=0, bytes_accessed=6 * 2**20, transcendentals=0),
    )(table, *places)


def offer_kernel(table, keys, values, *refs):
    outs, sem = refs[: 2 * W], refs[2 * W]
    copies = []
    for t, out in enumerate(outs):
        rows = pl.ds(pl.multiple_of(table[t] * BS, BS), BS)
        for half, source in enumerate((keys, values)):
            copies.append(pltpu.make_async_copy(source.at[rows, :], out.at[half], sem.at[t, half]))
    for copy in copies:
        copy.start()
    for copy in copies:
        copy.wait()


def offer(table, keys, values):
    return pl.pallas_call(
        offer_kernel,
        out_shape=(jax.ShapeDtypeStruct((2, BS, D), BF),) * (2 * W),
        in_specs=[SMEM, HBM, HBM],
        out_specs=(VMEM,) * (2 * W),
        scratch_shapes=[pltpu.SemaphoreType.DMA((2 * W, 2))],
        compiler_params=pltpu.CompilerParams(vmem_limit_bytes=4 * 2**20),
        cost_estimate=pl.CostEstimate(flops=0, bytes_accessed=2 * 2**20, transcendentals=0),
    )(table, keys, values)


def attend_pair(step, table, q_ref, g_ref, listed, att_ref, gq_ref, totals):
    low = lax.broadcasted_iota(jnp.int32, (BS, 128), 1) < 64
    last = (((1,), (1,)), ((), ()))
    first = (((0,), (0,)), ((), ()))
    s = step // PAIRS
    p = step % PAIRS
    cols = pl.ds(pl.multiple_of(p * 128, 128), 128)
    query = q_ref[s, :, cols]
    grad = g_ref[s, :, cols]
    zero = jnp.zeros_like(query)
    query2 = jnp.concatenate([jnp.where(low, query, zero), jnp.where(low, zero, query)], axis=0)
    grad2 = jnp.concatenate([jnp.where(low, grad, zero), jnp.where(low, zero, grad)], axis=0)
    keys = listed[s, 0, :, cols]
    values = listed[s, 1, :, cols]

    def own_heads(both):
        return jnp.concatenate([both[:64, :128], both[64:, 128:]], axis=0)

    scores = lax.dot_general(keys, query2, last, preferred_element_type=F32)
    highest = jnp.max(scores, axis=0, keepdims=True)
    raised = jnp.exp2((scores - highest) * (0.125 * math.log2(math.e)))
    weights = raised * (1.0 / jnp.sum(raised, axis=0, keepdims=True))
    weights_low = weights.astype(BF)
    mixture = own_heads(lax.dot_general(values, weights_low, first, preferred_element_type=F32))
    att_ref[s, :, cols] = mixture.T.astype(BF)
    product = mixture * grad.astype(F32).T
    carried = jnp.concatenate(
        [jnp.sum(product[:64], axis=0, keepdims=True), jnp.sum(product[64:], axis=0, keepdims=True)], axis=1
    )
    grad_weights = lax.dot_general(values, grad2, last, preferred_element_type=F32)
    grad_scores = ((weights * (grad_weights - carried)) * 0.125).astype(BF)
    grad_query = own_heads(lax.dot_general(keys, grad_scores, first, preferred_element_type=F32))
    gq_ref[s, :, cols] = grad_query.T.astype(BF)
    grad_key = jnp.dot(grad_scores, query2, preferred_element_type=F32)
    grad_value = jnp.dot(weights_low, grad2, preferred_element_type=F32)
    for j in range(KB):
        slot = table[2, s * KB + j]
        again = table[3, s * KB + j] == 0
        rows = slice(j * BS, (j + 1) * BS)
        for half, term in enumerate((grad_key, grad_value)):
            before = totals[slot, half, :, cols]
            totals[slot, half, :, cols] = jnp.where(again, before, 0.0) + term[rows]


def attend_kernel(table, q_ref, g_ref, *refs):
    own, near, places, picked = refs[0], refs[1:5], refs[5:13], refs[13]
    att_ref, gq_ref, own_out, far_out = refs[14:18]
    near_out, (listed, totals, sem) = refs[18:22], refs[22:]

    def bring(source, s, j):
        pltpu.make_async_copy(source, listed.at[s, :, pl.ds(j * BS, BS), :], sem.at[s]).start()

    for s in range(NB):
        bring(own.at[:, pl.ds(s * BS, BS), :], s, 0)
        for j in range(1, KB):
            code, place = table[0, s * KB + j], table[1, s * KB + j]
            rows = pl.ds(pl.multiple_of(place * BS, BS), BS)
            if j <= LOC:

                @pl.when(code == 0)
                def _():
                    bring(own.at[:, rows, :], s, j)

                for t in range(2 * W):

                    @pl.when(code == 1 + t)
                    def _():
                        bring(near[t], s, j)

            else:
                for t in range(8):

                    @pl.when(code == t)
                    def _():
                        bring(places[t].at[:, rows, :], s, j)

                @pl.when(code == 8)
                def _():
                    bring(picked.at[s * EXP + j - 1 - LOC], s, j)

    for s in range(NB):
        pltpu.make_async_copy(listed.at[s], listed.at[s], sem.at[s]).wait()

    def body(step, carry):
        attend_pair(step, table, q_ref, g_ref, listed, att_ref, gq_ref, totals)
        return carry

    lax.fori_loop(0, NB * PAIRS, body, 0, unroll=4)
    own_out[...] = totals[:NB].astype(BF)
    for t in range(2 * W):
        near_out[t][...] = totals[NB + t].astype(BF)
    far_out[...] = totals[NEAR:].astype(BF)


def attend(table, queries, cotangent, own, near, places, picked):
    return pl.pallas_call(
        attend_kernel,
        out_shape=(
            jax.ShapeDtypeStruct((NB, BS, D), BF),
            jax.ShapeDtypeStruct((NB, BS, D), BF),
            jax.ShapeDtypeStruct((NB, 2, BS, D), BF),
            jax.ShapeDtypeStruct((FAR, 2, BS, D), BF),
        )
        + (jax.ShapeDtypeStruct((2, BS, D), BF),) * (2 * W),
        in_specs=[SMEM, VMEM, VMEM] + [HBM] * 14,
        out_specs=(VMEM,) * (4 + 2 * W),
        scratch_shapes=[
            pltpu.VMEM((NB, 2, ROWS, D), BF),
            pltpu.VMEM((NEAR + FAR, 2, BS, D), F32),
            pltpu.SemaphoreType.DMA((NB,)),
        ],
        compiler_params=pltpu.CompilerParams(vmem_limit_bytes=32 * 2**20),
        cost_estimate=pl.CostEstimate(
            flops=12 * NB * BS * ROWS * D, bytes_accessed=12 * 2**20, transcendentals=NB * 8 * BS * ROWS
        ),
    )(table, queries, cotangent, own, *near, *places, picked)


def spread_kernel(count, table, mine, theirs, *outs):
    for n in range(count):
        out = outs[n]
        for s in range(NB):
            a, b = table[0, n * NB + s], table[1, n * NB + s]

            @pl.when((a < 0) & (b < 0))
            def _():
                out[s] = jnp.zeros((2, BS, D), BF)

            @pl.when((a >= 0) & (b < 0))
            def _():
                out[s] = mine[a]

            @pl.when((a < 0) & (b >= 0))
            def _():
                out[s] = theirs[b]

            @pl.when((a >= 0) & (b >= 0))
            def _():
                out[s] = (mine[a].astype(F32) + theirs[b].astype(F32)).astype(BF)


def spread(table, mine, theirs):
    count = table.shape[1] // NB
    return pl.pallas_call(
        functools.partial(spread_kernel, count),
        out_shape=tuple(jax.ShapeDtypeStruct((NB, 2, BS, D), BF) for _ in range(count)),
        in_specs=[SMEM, VMEM, VMEM],
        out_specs=(VMEM,) * count,
        compiler_params=pltpu.CompilerParams(vmem_limit_bytes=12 * 2**20),
        cost_estimate=pl.CostEstimate(flops=0, bytes_accessed=(3 + count) * 2**19, transcendentals=0),
    )(table, mine, theirs)


def close_kernel(table, near, theirs, from_a, from_b, *refs):
    returned, (gk_ref, gv_ref) = refs[:4], refs[4:]
    for s in range(NB):
        for half, out in enumerate((gk_ref, gv_ref)):
            total = near[s, half].astype(F32)
            for t in range(2 * W):
                total = total + jnp.where(table[t] == s, returned[t][half].astype(F32), 0.0)
            total = total + from_a[s, half].astype(F32) + from_b[s, half].astype(F32)
            b = table[4 + s]
            direct = theirs[jnp.maximum(b, 0), half].astype(F32)
            total = total + jnp.where(b >= 0, direct, 0.0)
            out[pl.ds(s * BS, BS), :] = total.astype(BF)


def close(table, near, theirs, from_a, from_b, returned):
    return pl.pallas_call(
        close_kernel,
        out_shape=(jax.ShapeDtypeStruct((NB * BS, D), BF),) * 2,
        in_specs=[SMEM] + [VMEM] * 8,
        out_specs=(VMEM, VMEM),
        compiler_params=pltpu.CompilerParams(vmem_limit_bytes=12 * 2**20),
        cost_estimate=pl.CostEstimate(flops=2**22, bytes_accessed=6 * 2**20, transcendentals=0),
    )(table, near, theirs, from_a, from_b, *returned)


def on_device(queries, keys, values, cotangent, local_list, far_list):
    groups = lax.axis_size("group")
    doms = lax.axis_size("dom")
    chips = groups // 2
    dom = lax.axis_index("dom").astype(jnp.int32)
    group = lax.axis_index("group").astype(jnp.int32)
    chip, core = group // 2, group % 2
    i32 = jnp.int32

    own = jnp.stack([keys, values])
    flow_a = [ring_step(own)]
    sibling = swap_cores(own)

    padded = jnp.pad(local_list, ((W * NB, W * NB), (0, 0)), constant_values=-1)
    around = lax.dynamic_slice_in_dim(padded, dom * NB, (2 * W + 1) * NB, 0).reshape(2 * W + 1, NB * LOC)
    given = jnp.max(jnp.where(around // NB == dom, around % NB, 0), axis=1).astype(i32)
    given = jnp.concatenate([given[:W], given[W + 1 :]])
    local = around[W].reshape(NB, LOC)
    holder = local // NB - dom
    near_code = jnp.where(holder == 0, 0, jnp.where(holder > 0, 3 - holder, 2 - holder))
    near_key = jnp.where(holder == 0, local % NB, NB - 1 + near_code)

    far_rows = far_list[0].reshape(groups, FAR)
    mine = lax.dynamic_index_in_dim(far_rows, group, 0, keepdims=False)
    theirs = lax.dynamic_index_in_dim(far_rows, group ^ 1, 0, keepdims=False)
    far_code = place_of(mine // NB, chip, core, chips)
    needed = place_of(theirs // NB, chip, 1 - core, chips) == PICKED
    sent = jnp.where(needed, place_of(theirs // NB, chip, core, chips), PICKED)
    pick_table = jnp.stack([sent, theirs % NB]).astype(i32)

    self_code = jnp.zeros((NB, 1), i32)
    self_key = jnp.arange(NB, dtype=i32)[:, None]
    codes = jnp.concatenate([self_code, near_code, far_code.reshape(NB, EXP)], axis=1).reshape(-1)
    slots = jnp.concatenate([self_key, local % NB, (mine % NB).reshape(NB, EXP)], axis=1).reshape(-1)
    far_key = (NEAR + first_of(mine)).reshape(NB, EXP)
    targets = jnp.concatenate([self_key, near_key, far_key], axis=1).reshape(-1)
    leads = first_of(targets) == jnp.arange(ENTRIES, dtype=i32)
    table = jnp.stack([codes, slots, targets, leads.astype(i32)]).astype(i32)
    steps = [(4, 0), (3, 1), (3, 0), (2, 1), (2, 0), (1, 1), (1, 0)]
    direction = 1 - 2 * core
    wanted = []
    for distance, side in steps:
        cluster = ((chip + direction * distance) % chips) * 2 + jnp.where(side == 0, core, 1 - core)
        wanted += [cluster * NB, cluster * NB + 1]
    wanted += [group * NB, group * NB + 1]
    wanted = jnp.stack(wanted).astype(i32)
    hits = jnp.stack([slot_in(mine, wanted), slot_in(theirs, wanted)])
    last = jnp.concatenate([given, hits[1, 7 * NB :]]).astype(i32)
    tables = (given, pick_table, table, hits[:, : 2 * NB], hits[:, 2 * NB : 7 * NB], last)
    flow_a[0], sibling, tables = lax.optimization_barrier((flow_a[0], sibling, tables))
    given, pick_table, table, hits_first, hits_rest, last = tables

    offered = offer(given, keys, values)
    flow_b = [ring_step(sibling)]
    near = [None, None, shifted(offered[2], OFFSETS[2]), shifted(offered[3], OFFSETS[3])]
    flow_a[0], near[2], near[3] = lax.optimization_barrier((flow_a[0], near[2], near[3]))
    flow_a.append(ring_step(flow_a[0]))
    behind = lax.optimization_barrier((offered[0], offered[1], near[2], near[3]))
    near = [shifted(behind[0], OFFSETS[0]), shifted(behind[1], OFFSETS[1]), behind[2], behind[3]]
    flow_b.append(ring_step(flow_b[0]))
    flow_a[1], near = lax.optimization_barrier((flow_a[1], near))
    flow_a.append(ring_step(flow_a[1]))
    flow_b.append(ring_step(flow_b[1]))
    flow_a.append(ring_step(flow_a[2]))

    picked = swap_cores(pick(pick_table, [sibling] + flow_a + flow_b))
    attended, grad_queries, own_terms, far_terms, *near_terms = attend(
        table,
        queries.reshape(NB, BS, D),
        cotangent.reshape(NB, BS, D),
        own,
        near,
        [sibling] + flow_a + flow_b,
        picked,
    )

    sibling_terms = swap_cores(far_terms)
    start_a, start_b = spread(hits_first, far_terms, sibling_terms)
    a3, b2, a2, b1, a1 = spread(hits_rest, far_terms, sibling_terms)

    def joined(x, y):
        return (x.astype(F32) + y.astype(F32)).astype(BF)

    back_a = ring_step(start_a)
    back_b = ring_step(start_b)
    returned = [shifted(near_terms[t], -OFFSETS[t]) for t in (0, 1)]
    back_a, *returned = lax.optimization_barrier((back_a, *returned))
    back_a = ring_step(joined(back_a, a3))
    back_b = ring_step(joined(back_b, b2))
    back_a, *behind = lax.optimization_barrier((back_a, near_terms[2], near_terms[3], *returned))
    returned = behind[2:] + [shifted(behind[t - 2], -OFFSETS[t]) for t in (2, 3)]
    back_a = ring_step(joined(back_a, a2))
    back_b = ring_step(joined(back_b, b1))
    back_a, *returned = lax.optimization_barrier((back_a, *returned))
    back_a = ring_step(joined(back_a, a1))
    back_b = swap_cores(back_b)

    grad_keys, grad_values = close(last, own_terms, sibling_terms, back_a, back_b, returned)
    return (attended.reshape(NB * BS, D), grad_queries.reshape(NB * BS, D), grad_keys, grad_values)


def solution(mesh):
    rows = P(("group", "dom"), None)
    return jax.shard_map(
        on_device,
        mesh=mesh,
        in_specs=(rows, rows, rows, rows, P("group", None), P("dom", None, None)),
        out_specs=(rows, rows, rows, rows),
        check_vma=False,
    )
```

```python
import functools
import math

import jax
import jax.numpy as jnp
from jax import lax
from jax.experimental import pallas as pl
from jax.experimental.pallas import tpu as pltpu
from jax.sharding import PartitionSpec as P

D = 512
BS = 128
NB = 2
LOC = 3
EXP = 3
W = 2
KB = 1 + LOC + EXP
ENTRIES = NB * KB
ROWS = KB * BS
FAR = NB * EXP
NEAR = NB + 2 * W
PAIRS = D // 128
BF = jnp.bfloat16
F32 = jnp.float32
OFFSETS = (-2, -1, 1, 2)

HBM = pl.BlockSpec(memory_space=pltpu.HBM)
VMEM = pl.BlockSpec(memory_space=pltpu.VMEM)
SMEM = pl.BlockSpec(memory_space=pltpu.SMEM)

SIBLING, FLOW_A, FLOW_B, PICKED = 0, 0, 4, 8


def ring_step(array):
    size = lax.axis_size("group")
    return lax.ppermute(array, "group", [(g, (g + (2 if g % 2 == 0 else -2)) % size) for g in range(size)])


def swap_cores(array):
    size = lax.axis_size("group")
    return lax.ppermute(array, "group", [(g, g ^ 1) for g in range(size)])


def shifted(array, by):
    size = lax.axis_size("dom")
    return lax.ppermute(array, "dom", [(i, i + by) for i in range(size) if 0 <= i + by < size])


def place_of(cluster, chip, core, chips):
    other_chip, other_core = cluster // 2, cluster % 2
    distance = jnp.where(core == 0, chip - other_chip, other_chip - chip) % chips
    same = other_core == core
    half = chips // 2
    here = jnp.where(same, FLOW_A + distance, FLOW_B + distance)
    held = jnp.where(same, distance <= half, distance < half)
    return jnp.where(distance == 0, SIBLING, jnp.where(held, here, PICKED))


def first_of(values):
    order = jnp.arange(values.shape[0], dtype=jnp.int32)
    same = values[:, None] == values[None, :]
    return jnp.min(jnp.where(same, order[None, :], values.shape[0]), axis=1)


def slot_in(values, wanted):
    order = jnp.arange(values.shape[0], dtype=jnp.int32)
    hit = values[None, :] == wanted[:, None]
    found = jnp.min(jnp.where(hit, order[None, :], values.shape[0]), axis=1)
    return jnp.where(found == values.shape[0], -1, found).astype(jnp.int32)


def pick_kernel(table, *refs):
    places, out, sem = refs[:8], refs[8], refs[9]
    copies = []
    for t in range(FAR):
        for code, place in enumerate(places):

            @pl.when(table[0, t] == code)
            def _():
                rows = pl.ds(pl.multiple_of(table[1, t] * BS, BS), BS)
                pltpu.make_async_copy(place.at[:, rows, :], out.at[t], sem.at[t]).start()

    for t in range(FAR):

        @pl.when(table[0, t] < 8)
        def _():
            pltpu.make_async_copy(places[0].at[:, pl.ds(0, BS), :], out.at[t], sem.at[t]).wait()


def pick(table, places):
    return pl.pallas_call(
        pick_kernel,
        out_shape=jax.ShapeDtypeStruct((FAR, 2, BS, D), BF),
        in_specs=[SMEM] + [HBM] * 8,
        out_specs=VMEM,
        scratch_shapes=[pltpu.SemaphoreType.DMA((FAR,))],
        compiler_params=pltpu.CompilerParams(vmem_limit_bytes=4 * 2**20),
        cost_estimate=pl.CostEstimate(flops=0, bytes_accessed=6 * 2**20, transcendentals=0),
    )(table, *places)


def offer_kernel(table, keys, values, *refs):
    outs, sem = refs[: 2 * W], refs[2 * W]
    copies = []
    for t, out in enumerate(outs):
        rows = pl.ds(pl.multiple_of(table[t] * BS, BS), BS)
        for half, source in enumerate((keys, values)):
            copies.append(pltpu.make_async_copy(source.at[rows, :], out.at[half], sem.at[t, half]))
    for copy in copies:
        copy.start()
    for copy in copies:
        copy.wait()


def offer(table, keys, values):
    return pl.pallas_call(
        offer_kernel,
        out_shape=(jax.ShapeDtypeStruct((2, BS, D), BF),) * (2 * W),
        in_specs=[SMEM, HBM, HBM],
        out_specs=(VMEM,) * (2 * W),
        scratch_shapes=[pltpu.SemaphoreType.DMA((2 * W, 2))],
        compiler_params=pltpu.CompilerParams(vmem_limit_bytes=4 * 2**20),
        cost_estimate=pl.CostEstimate(flops=0, bytes_accessed=2 * 2**20, transcendentals=0),
    )(table, keys, values)


def attend_pair(step, table, q_ref, g_ref, listed, att_ref, gq_ref, totals):
    low = lax.broadcasted_iota(jnp.int32, (BS, 128), 1) < 64
    last = (((1,), (1,)), ((), ()))
    first = (((0,), (0,)), ((), ()))
    s = step // PAIRS
    p = step % PAIRS
    cols = pl.ds(pl.multiple_of(p * 128, 128), 128)
    query = q_ref[s, :, cols]
    grad = g_ref[s, :, cols]
    zero = jnp.zeros_like(query)
    query2 = jnp.concatenate([jnp.where(low, query, zero), jnp.where(low, zero, query)], axis=0)
    grad2 = jnp.concatenate([jnp.where(low, grad, zero), jnp.where(low, zero, grad)], axis=0)
    keys = listed[s, 0, :, cols]
    values = listed[s, 1, :, cols]

    def own_heads(both):
        return jnp.concatenate([both[:64, :128], both[64:, 128:]], axis=0)

    scores = lax.dot_general(keys, query2, last, preferred_element_type=F32)
    highest = jnp.max(scores, axis=0, keepdims=True)
    raised = jnp.exp2((scores - highest) * (0.125 * math.log2(math.e)))
    weights = raised * (1.0 / jnp.sum(raised, axis=0, keepdims=True))
    weights_low = weights.astype(BF)
    mixture = own_heads(lax.dot_general(values, weights_low, first, preferred_element_type=F32))
    att_ref[s, :, cols] = mixture.T.astype(BF)
    product = mixture * grad.astype(F32).T
    carried = jnp.concatenate(
        [jnp.sum(product[:64], axis=0, keepdims=True), jnp.sum(product[64:], axis=0, keepdims=True)], axis=1
    )
    grad_weights = lax.dot_general(values, grad2, last, preferred_element_type=F32)
    grad_scores = ((weights * (grad_weights - carried)) * 0.125).astype(BF)
    grad_query = own_heads(lax.dot_general(keys, grad_scores, first, preferred_element_type=F32))
    gq_ref[s, :, cols] = grad_query.T.astype(BF)
    grad_key = jnp.dot(grad_scores, query2, preferred_element_type=F32)
    grad_value = jnp.dot(weights_low, grad2, preferred_element_type=F32)
    for j in range(KB):
        slot = table[2, s * KB + j]
        again = table[3, s * KB + j] == 0
        rows = slice(j * BS, (j + 1) * BS)
        for half, term in enumerate((grad_key, grad_value)):
            before = totals[slot, half, :, cols]
            totals[slot, half, :, cols] = jnp.where(again, before, 0.0) + term[rows]


def attend_kernel(table, q_ref, g_ref, *refs):
    own, near, places, picked = refs[0], refs[1:5], refs[5:13], refs[13]
    att_ref, gq_ref, own_out, far_out = refs[14:18]
    near_out, (listed, totals, sem) = refs[18:22], refs[22:]

    def bring(source, s, j):
        pltpu.make_async_copy(source, listed.at[s, :, pl.ds(j * BS, BS), :], sem.at[s]).start()

    for s in range(NB):
        bring(own.at[:, pl.ds(s * BS, BS), :], s, 0)
        for j in range(1, KB):
            code, place = table[0, s * KB + j], table[1, s * KB + j]
            rows = pl.ds(pl.multiple_of(place * BS, BS), BS)
            if j <= LOC:

                @pl.when(code == 0)
                def _():
                    bring(own.at[:, rows, :], s, j)

                for t in range(2 * W):

                    @pl.when(code == 1 + t)
                    def _():
                        bring(near[t], s, j)

            else:
                for t in range(8):

                    @pl.when(code == t)
                    def _():
                        bring(places[t].at[:, rows, :], s, j)

                @pl.when(code == 8)
                def _():
                    bring(picked.at[s * EXP + j - 1 - LOC], s, j)

    for s in range(NB):
        pltpu.make_async_copy(listed.at[s], listed.at[s], sem.at[s]).wait()

    def body(step, carry):
        attend_pair(step, table, q_ref, g_ref, listed, att_ref, gq_ref, totals)
        return carry

    lax.fori_loop(0, NB * PAIRS, body, 0, unroll=4)
    own_out[...] = totals[:NB].astype(BF)
    for t in range(2 * W):
        near_out[t][...] = totals[NB + t].astype(BF)
    far_out[...] = totals[NEAR:].astype(BF)


def attend(table, queries, cotangent, own, near, places, picked):
    return pl.pallas_call(
        attend_kernel,
        out_shape=(
            jax.ShapeDtypeStruct((NB, BS, D), BF),
            jax.ShapeDtypeStruct((NB, BS, D), BF),
            jax.ShapeDtypeStruct((NB, 2, BS, D), BF),
            jax.ShapeDtypeStruct((FAR, 2, BS, D), BF),
        )
        + (jax.ShapeDtypeStruct((2, BS, D), BF),) * (2 * W),
        in_specs=[SMEM, VMEM, VMEM] + [HBM] * 14,
        out_specs=(VMEM,) * (4 + 2 * W),
        scratch_shapes=[
            pltpu.VMEM((NB, 2, ROWS, D), BF),
            pltpu.VMEM((NEAR + FAR, 2, BS, D), F32),
            pltpu.SemaphoreType.DMA((NB,)),
        ],
        compiler_params=pltpu.CompilerParams(vmem_limit_bytes=32 * 2**20),
        cost_estimate=pl.CostEstimate(
            flops=12 * NB * BS * ROWS * D, bytes_accessed=12 * 2**20, transcendentals=NB * 8 * BS * ROWS
        ),
    )(table, queries, cotangent, own, *near, *places, picked)


def spread_kernel(count, table, mine, theirs, *outs):
    for n in range(count):
        out = outs[n]
        for s in range(NB):
            a, b = table[0, n * NB + s], table[1, n * NB + s]

            @pl.when((a < 0) & (b < 0))
            def _():
                out[s] = jnp.zeros((2, BS, D), BF)

            @pl.when((a >= 0) & (b < 0))
            def _():
                out[s] = mine[a]

            @pl.when((a < 0) & (b >= 0))
            def _():
                out[s] = theirs[b]

            @pl.when((a >= 0) & (b >= 0))
            def _():
                out[s] = (mine[a].astype(F32) + theirs[b].astype(F32)).astype(BF)


def spread(table, mine, theirs):
    count = table.shape[1] // NB
    return pl.pallas_call(
        functools.partial(spread_kernel, count),
        out_shape=tuple(jax.ShapeDtypeStruct((NB, 2, BS, D), BF) for _ in range(count)),
        in_specs=[SMEM, VMEM, VMEM],
        out_specs=(VMEM,) * count,
        compiler_params=pltpu.CompilerParams(vmem_limit_bytes=12 * 2**20),
        cost_estimate=pl.CostEstimate(flops=0, bytes_accessed=(3 + count) * 2**19, transcendentals=0),
    )(table, mine, theirs)


def close_kernel(table, near, theirs, from_a, from_b, *refs):
    returned, (gk_ref, gv_ref) = refs[:4], refs[4:]
    for s in range(NB):
        for half, out in enumerate((gk_ref, gv_ref)):
            total = near[s, half].astype(F32)
            for t in range(2 * W):
                total = total + jnp.where(table[t] == s, returned[t][half].astype(F32), 0.0)
            total = total + from_a[s, half].astype(F32) + from_b[s, half].astype(F32)
            b = table[4 + s]
            direct = theirs[jnp.maximum(b, 0), half].astype(F32)
            total = total + jnp.where(b >= 0, direct, 0.0)
            out[pl.ds(s * BS, BS), :] = total.astype(BF)


def close(table, near, theirs, from_a, from_b, returned):
    return pl.pallas_call(
        close_kernel,
        out_shape=(jax.ShapeDtypeStruct((NB * BS, D), BF),) * 2,
        in_specs=[SMEM] + [VMEM] * 8,
        out_specs=(VMEM, VMEM),
        compiler_params=pltpu.CompilerParams(vmem_limit_bytes=12 * 2**20),
        cost_estimate=pl.CostEstimate(flops=2**22, bytes_accessed=6 * 2**20, transcendentals=0),
    )(table, near, theirs, from_a, from_b, *returned)


def on_device(queries, keys, values, cotangent, local_list, far_list):
    groups = lax.axis_size("group")
    doms = lax.axis_size("dom")
    chips = groups // 2
    dom = lax.axis_index("dom").astype(jnp.int32)
    group = lax.axis_index("group").astype(jnp.int32)
    chip, core = group // 2, group % 2
    i32 = jnp.int32

    own = jnp.stack([keys, values])
    flow_a = [ring_step(own)]
    sibling = swap_cores(own)

    padded = jnp.pad(local_list, ((W * NB, W * NB), (0, 0)), constant_values=-1)
    around = lax.dynamic_slice_in_dim(padded, dom * NB, (2 * W + 1) * NB, 0).reshape(2 * W + 1, NB * LOC)
    given = jnp.max(jnp.where(around // NB == dom, around % NB, 0), axis=1).astype(i32)
    given = jnp.concatenate([given[:W], given[W + 1 :]])
    local = around[W].reshape(NB, LOC)
    holder = local // NB - dom
    near_code = jnp.where(holder == 0, 0, jnp.where(holder > 0, 3 - holder, 2 - holder))
    near_key = jnp.where(holder == 0, local % NB, NB - 1 + near_code)

    far_rows = far_list[0].reshape(groups, FAR)
    mine = lax.dynamic_index_in_dim(far_rows, group, 0, keepdims=False)
    theirs = lax.dynamic_index_in_dim(far_rows, group ^ 1, 0, keepdims=False)
    far_code = place_of(mine // NB, chip, core, chips)
    needed = place_of(theirs // NB, chip, 1 - core, chips) == PICKED
    sent = jnp.where(needed, place_of(theirs // NB, chip, core, chips), PICKED)
    pick_table = jnp.stack([sent, theirs % NB]).astype(i32)

    self_code = jnp.zeros((NB, 1), i32)
    self_key = jnp.arange(NB, dtype=i32)[:, None]
    codes = jnp.concatenate([self_code, near_code, far_code.reshape(NB, EXP)], axis=1).reshape(-1)
    slots = jnp.concatenate([self_key, local % NB, (mine % NB).reshape(NB, EXP)], axis=1).reshape(-1)
    far_key = (NEAR + first_of(mine)).reshape(NB, EXP)
    targets = jnp.concatenate([self_key, near_key, far_key], axis=1).reshape(-1)
    leads = first_of(targets) == jnp.arange(ENTRIES, dtype=i32)
    table = jnp.stack([codes, slots, targets, leads.astype(i32)]).astype(i32)
    steps = [(4, 0), (3, 1), (3, 0), (2, 1), (2, 0), (1, 1), (1, 0)]
    direction = 1 - 2 * core
    wanted = []
    for distance, side in steps:
        cluster = ((chip + direction * distance) % chips) * 2 + jnp.where(side == 0, core, 1 - core)
        wanted += [cluster * NB, cluster * NB + 1]
    wanted += [group * NB, group * NB + 1]
    wanted = jnp.stack(wanted).astype(i32)
    hits = jnp.stack([slot_in(mine, wanted), slot_in(theirs, wanted)])
    last = jnp.concatenate([given, hits[1, 7 * NB :]]).astype(i32)
    tables = (given, pick_table, table, hits[:, : 2 * NB], hits[:, 2 * NB : 7 * NB], last)
    sibling, tables = lax.optimization_barrier((sibling, tables))
    given, pick_table, table, hits_first, hits_rest, last = tables

    flow_b = [ring_step(sibling)]
    flow_a.append(ring_step(flow_a[0]))
    offered = offer(given, keys, values)
    flow_b.append(ring_step(flow_b[0]))
    up = [shifted(offered[t], OFFSETS[t]) for t in (2, 3)]
    flow_a[1], *up = lax.optimization_barrier((flow_a[1], *up))
    flow_a.append(ring_step(flow_a[1]))
    behind = lax.optimization_barrier((offered[0], offered[1], *up))
    up = list(behind[2:])
    down = [shifted(behind[t], OFFSETS[t]) for t in (0, 1)]
    near = down + up
    flow_b.append(ring_step(flow_b[1]))
    flow_a[2], near = lax.optimization_barrier((flow_a[2], near))
    flow_a.append(ring_step(flow_a[2]))

    picked = swap_cores(pick(pick_table, [sibling] + flow_a + flow_b))
    attended, grad_queries, own_terms, far_terms, *near_terms = attend(
        table,
        queries.reshape(NB, BS, D),
        cotangent.reshape(NB, BS, D),
        own,
        near,
        [sibling] + flow_a + flow_b,
        picked,
    )

    sibling_terms = swap_cores(far_terms)
    start_a, start_b = spread(hits_first, far_terms, sibling_terms)
    a3, b2, a2, b1, a1 = spread(hits_rest, far_terms, sibling_terms)

    def joined(x, y):
        return (x.astype(F32) + y.astype(F32)).astype(BF)

    back_a = ring_step(start_a)
    back_b = ring_step(start_b)
    back_a = ring_step(joined(back_a, a3))
    back_b = ring_step(joined(back_b, b2))
    returned = [shifted(near_terms[t], -OFFSETS[t]) for t in (0, 1)]
    back_a, *behind = lax.optimization_barrier((back_a, near_terms[2], near_terms[3], *returned))
    returned = behind[2:] + [shifted(behind[t - 2], -OFFSETS[t]) for t in (2, 3)]
    back_a = ring_step(joined(back_a, a2))
    back_b = ring_step(joined(back_b, b1))
    back_a = ring_step(joined(back_a, a1))
    back_b = swap_cores(back_b)

    grad_keys, grad_values = close(last, own_terms, sibling_terms, back_a, back_b, returned)
    return (attended.reshape(NB * BS, D), grad_queries.reshape(NB * BS, D), grad_keys, grad_values)


def solution(mesh):
    rows = P(("group", "dom"), None)
    return jax.shard_map(
        on_device,
        mesh=mesh,
        in_specs=(rows, rows, rows, rows, P("group", None), P("dom", None, None)),
        out_specs=(rows, rows, rows, rows),
        check_vma=False,
    )
```

```python
import functools
import math

import jax
import jax.numpy as jnp
from jax import lax
from jax.experimental import pallas as pl
from jax.experimental.pallas import tpu as pltpu
from jax.sharding import PartitionSpec as P

D = 512
BS = 128
NB = 2
LOC = 3
EXP = 3
W = 2
KB = 1 + LOC + EXP
ENTRIES = NB * KB
ROWS = KB * BS
FAR = NB * EXP
NEAR = NB + 2 * W
PAIRS = D // 128
BF = jnp.bfloat16
F32 = jnp.float32

HBM = pl.BlockSpec(memory_space=pltpu.HBM)
VMEM = pl.BlockSpec(memory_space=pltpu.VMEM)
SMEM = pl.BlockSpec(memory_space=pltpu.SMEM)

SIBLING, FLOW_A, FLOW_B, PICKED = 0, 0, 4, 8


def ring_step(array):
    size = lax.axis_size("group")
    return lax.ppermute(array, "group", [(g, (g + (2 if g % 2 == 0 else -2)) % size) for g in range(size)])


def swap_cores(array):
    size = lax.axis_size("group")
    return lax.ppermute(array, "group", [(g, g ^ 1) for g in range(size)])


def dom_step(array, by):
    groups, doms = lax.axis_size("group"), lax.axis_size("dom")
    pairs = []
    for g in range(groups):
        for i in range(doms):
            to = i + (by if g % 2 == 0 else -by)
            if 0 <= to < doms:
                pairs.append((g * doms + i, g * doms + to))
    return lax.ppermute(array, ("group", "dom"), pairs)


def place_of(cluster, chip, core, chips):
    other_chip, other_core = cluster // 2, cluster % 2
    distance = jnp.where(core == 0, chip - other_chip, other_chip - chip) % chips
    same = other_core == core
    half = chips // 2
    here = jnp.where(same, FLOW_A + distance, FLOW_B + distance)
    held = jnp.where(same, distance <= half, distance < half)
    return jnp.where(distance == 0, SIBLING, jnp.where(held, here, PICKED))


def first_of(values):
    order = jnp.arange(values.shape[0], dtype=jnp.int32)
    same = values[:, None] == values[None, :]
    return jnp.min(jnp.where(same, order[None, :], values.shape[0]), axis=1)


def slot_in(values, wanted):
    order = jnp.arange(values.shape[0], dtype=jnp.int32)
    hit = values[None, :] == wanted[:, None]
    found = jnp.min(jnp.where(hit, order[None, :], values.shape[0]), axis=1)
    return jnp.where(found == values.shape[0], -1, found).astype(jnp.int32)


def pick_kernel(table, *refs):
    places, out, sem = refs[:8], refs[8], refs[9]
    copies = []
    for t in range(FAR):
        for code, place in enumerate(places):

            @pl.when(table[0, t] == code)
            def _():
                rows = pl.ds(pl.multiple_of(table[1, t] * BS, BS), BS)
                pltpu.make_async_copy(place.at[:, rows, :], out.at[t], sem.at[t]).start()

    for t in range(FAR):

        @pl.when(table[0, t] < 8)
        def _():
            pltpu.make_async_copy(places[0].at[:, pl.ds(0, BS), :], out.at[t], sem.at[t]).wait()


def pick(table, places):
    return pl.pallas_call(
        pick_kernel,
        out_shape=jax.ShapeDtypeStruct((FAR, 2, BS, D), BF),
        in_specs=[SMEM] + [HBM] * 8,
        out_specs=VMEM,
        scratch_shapes=[pltpu.SemaphoreType.DMA((FAR,))],
        compiler_params=pltpu.CompilerParams(vmem_limit_bytes=4 * 2**20),
        cost_estimate=pl.CostEstimate(flops=0, bytes_accessed=6 * 2**20, transcendentals=0),
    )(table, *places)


def offer_kernel(table, keys, values, *refs):
    outs, sem = refs[:2], refs[2]
    copies = []
    for t in range(2 * W):
        rows = pl.ds(pl.multiple_of(table[t] * BS, BS), BS)
        for half, source in enumerate((keys, values)):
            target = outs[t // W].at[t % W, half]
            copies.append(pltpu.make_async_copy(source.at[rows, :], target, sem.at[t, half]))
    for copy in copies:
        copy.start()
    for copy in copies:
        copy.wait()


def offer(table, keys, values):
    return pl.pallas_call(
        offer_kernel,
        out_shape=(jax.ShapeDtypeStruct((W, 2, BS, D), BF),) * 2,
        in_specs=[SMEM, HBM, HBM],
        out_specs=(VMEM,) * 2,
        scratch_shapes=[pltpu.SemaphoreType.DMA((2 * W, 2))],
        compiler_params=pltpu.CompilerParams(vmem_limit_bytes=4 * 2**20),
        cost_estimate=pl.CostEstimate(flops=0, bytes_accessed=2 * 2**20, transcendentals=0),
    )(table, keys, values)


def attend_pair(step, table, q_ref, g_ref, listed, att_ref, gq_ref, totals):
    low = lax.broadcasted_iota(jnp.int32, (BS, 128), 1) < 64
    last = (((1,), (1,)), ((), ()))
    first = (((0,), (0,)), ((), ()))
    s = step // PAIRS
    p = step % PAIRS
    cols = pl.ds(pl.multiple_of(p * 128, 128), 128)
    query = q_ref[s, :, cols]
    grad = g_ref[s, :, cols]
    zero = jnp.zeros_like(query)
    query2 = jnp.concatenate([jnp.where(low, query, zero), jnp.where(low, zero, query)], axis=0)
    grad2 = jnp.concatenate([jnp.where(low, grad, zero), jnp.where(low, zero, grad)], axis=0)
    keys = listed[s, 0, :, cols]
    values = listed[s, 1, :, cols]

    def own_heads(both):
        return jnp.concatenate([both[:64, :128], both[64:, 128:]], axis=0)

    scores = lax.dot_general(keys, query2, last, preferred_element_type=F32)
    highest = jnp.max(scores, axis=0, keepdims=True)
    raised = jnp.exp2((scores - highest) * (0.125 * math.log2(math.e)))
    weights = raised * (1.0 / jnp.sum(raised, axis=0, keepdims=True))
    weights_low = weights.astype(BF)
    mixture = own_heads(lax.dot_general(values, weights_low, first, preferred_element_type=F32))
    att_ref[s, :, cols] = mixture.T.astype(BF)
    product = mixture * grad.astype(F32).T
    carried = jnp.concatenate(
        [jnp.sum(product[:64], axis=0, keepdims=True), jnp.sum(product[64:], axis=0, keepdims=True)], axis=1
    )
    grad_weights = lax.dot_general(values, grad2, last, preferred_element_type=F32)
    grad_scores = ((weights * (grad_weights - carried)) * 0.125).astype(BF)
    grad_query = own_heads(lax.dot_general(keys, grad_scores, first, preferred_element_type=F32))
    gq_ref[s, :, cols] = grad_query.T.astype(BF)
    grad_key = jnp.dot(grad_scores, query2, preferred_element_type=F32)
    grad_value = jnp.dot(weights_low, grad2, preferred_element_type=F32)
    for j in range(KB):
        slot = table[2, s * KB + j]
        again = table[3, s * KB + j] == 0
        rows = slice(j * BS, (j + 1) * BS)
        for half, term in enumerate((grad_key, grad_value)):
            before = totals[slot, half, :, cols]
            totals[slot, half, :, cols] = jnp.where(again, before, 0.0) + term[rows]


def attend_kernel(table, q_ref, g_ref, *refs):
    own, (one, two, other), places, picked = refs[0], refs[1:4], refs[4:12], refs[12]
    near = (one.at[0], two.at[0], other.at[0], other.at[1])
    att_ref, gq_ref, own_out, far_out, keep_out, give_out, listed, totals, sem = refs[13:]

    def bring(source, s, j):
        pltpu.make_async_copy(source, listed.at[s, :, pl.ds(j * BS, BS), :], sem.at[s]).start()

    for s in range(NB):
        bring(own.at[:, pl.ds(s * BS, BS), :], s, 0)
        for j in range(1, KB):
            code, place = table[0, s * KB + j], table[1, s * KB + j]
            rows = pl.ds(pl.multiple_of(place * BS, BS), BS)
            if j <= LOC:

                @pl.when(code == 0)
                def _():
                    bring(own.at[:, rows, :], s, j)

                for t in range(2 * W):

                    @pl.when(code == 1 + t)
                    def _():
                        bring(near[t], s, j)

            else:
                for t in range(8):

                    @pl.when(code == t)
                    def _():
                        bring(places[t].at[:, rows, :], s, j)

                @pl.when(code == 8)
                def _():
                    bring(picked.at[s * EXP + j - 1 - LOC], s, j)

    for s in range(NB):
        pltpu.make_async_copy(listed.at[s], listed.at[s], sem.at[s]).wait()

    def body(step, carry):
        attend_pair(step, table, q_ref, g_ref, listed, att_ref, gq_ref, totals)
        return carry

    lax.fori_loop(0, NB * PAIRS, body, 0, unroll=4)
    own_out[...] = totals[:NB].astype(BF)
    keep_out[...] = totals[NB : NB + W].astype(BF)
    give_out[...] = totals[NB + W : NEAR].astype(BF)
    far_out[...] = totals[NEAR:].astype(BF)


def attend(table, queries, cotangent, own, near, places, picked):
    return pl.pallas_call(
        attend_kernel,
        out_shape=(
            jax.ShapeDtypeStruct((NB, BS, D), BF),
            jax.ShapeDtypeStruct((NB, BS, D), BF),
            jax.ShapeDtypeStruct((NB, 2, BS, D), BF),
            jax.ShapeDtypeStruct((FAR, 2, BS, D), BF),
        )
        + (jax.ShapeDtypeStruct((W, 2, BS, D), BF),) * 2,
        in_specs=[SMEM, VMEM, VMEM] + [HBM] * 13,
        out_specs=(VMEM,) * 6,
        scratch_shapes=[
            pltpu.VMEM((NB, 2, ROWS, D), BF),
            pltpu.VMEM((NEAR + FAR, 2, BS, D), F32),
            pltpu.SemaphoreType.DMA((NB,)),
        ],
        compiler_params=pltpu.CompilerParams(vmem_limit_bytes=32 * 2**20),
        cost_estimate=pl.CostEstimate(
            flops=12 * NB * BS * ROWS * D, bytes_accessed=12 * 2**20, transcendentals=NB * 8 * BS * ROWS
        ),
    )(table, queries, cotangent, own, *near, *places, picked)


def spread_kernel(count, table, mine, theirs, *outs):
    for n in range(count):
        out = outs[n]
        for s in range(NB):
            a, b = table[0, n * NB + s], table[1, n * NB + s]

            @pl.when((a < 0) & (b < 0))
            def _():
                out[s] = jnp.zeros((2, BS, D), BF)

            @pl.when((a >= 0) & (b < 0))
            def _():
                out[s] = mine[a]

            @pl.when((a < 0) & (b >= 0))
            def _():
                out[s] = theirs[b]

            @pl.when((a >= 0) & (b >= 0))
            def _():
                out[s] = (mine[a].astype(F32) + theirs[b].astype(F32)).astype(BF)


def spread(table, mine, theirs):
    count = table.shape[1] // NB
    return pl.pallas_call(
        functools.partial(spread_kernel, count),
        out_shape=tuple(jax.ShapeDtypeStruct((NB, 2, BS, D), BF) for _ in range(count)),
        in_specs=[SMEM, VMEM, VMEM],
        out_specs=(VMEM,) * count,
        compiler_params=pltpu.CompilerParams(vmem_limit_bytes=12 * 2**20),
        cost_estimate=pl.CostEstimate(flops=0, bytes_accessed=(3 + count) * 2**19, transcendentals=0),
    )(table, mine, theirs)


def close_kernel(table, near, theirs, from_a, from_b, *refs):
    (one, two, other), (gk_ref, gv_ref) = refs[:3], refs[3:]
    returned = (one.at[0], two.at[0], other.at[0], other.at[1])
    for s in range(NB):
        for half, out in enumerate((gk_ref, gv_ref)):
            total = near[s, half].astype(F32)
            for t in range(2 * W):
                total = total + jnp.where(table[t] == s, returned[t][half].astype(F32), 0.0)
            total = total + from_a[s, half].astype(F32) + from_b[s, half].astype(F32)
            b = table[4 + s]
            direct = theirs[jnp.maximum(b, 0), half].astype(F32)
            total = total + jnp.where(b >= 0, direct, 0.0)
            out[pl.ds(s * BS, BS), :] = total.astype(BF)


def close(table, near, theirs, from_a, from_b, returned):
    return pl.pallas_call(
        close_kernel,
        out_shape=(jax.ShapeDtypeStruct((NB * BS, D), BF),) * 2,
        in_specs=[SMEM] + [VMEM] * 7,
        out_specs=(VMEM, VMEM),
        compiler_params=pltpu.CompilerParams(vmem_limit_bytes=12 * 2**20),
        cost_estimate=pl.CostEstimate(flops=2**22, bytes_accessed=6 * 2**20, transcendentals=0),
    )(table, near, theirs, from_a, from_b, *returned)


def on_device(queries, keys, values, cotangent, local_list, far_list):
    groups = lax.axis_size("group")
    doms = lax.axis_size("dom")
    chips = groups // 2
    dom = lax.axis_index("dom").astype(jnp.int32)
    group = lax.axis_index("group").astype(jnp.int32)
    chip, core = group // 2, group % 2
    i32 = jnp.int32

    own = jnp.stack([keys, values])
    flow_a = [ring_step(own)]
    sibling = swap_cores(own)

    padded = jnp.pad(local_list, ((W * NB, W * NB), (0, 0)), constant_values=-1)
    around = lax.dynamic_slice_in_dim(padded, dom * NB, (2 * W + 1) * NB, 0).reshape(2 * W + 1, NB * LOC)
    given = jnp.max(jnp.where(around // NB == dom, around % NB, 0), axis=1).astype(i32)
    up, down = given[W + 1 :], given[:W][::-1]
    given = jnp.where(core == 0, jnp.concatenate([up, down]), jnp.concatenate([down, up]))
    local = around[W].reshape(NB, LOC)
    holder = local // NB - dom
    direct = (holder < 0) == (core == 0)
    near_code = jnp.where(holder == 0, 0, jnp.abs(holder) + jnp.where(direct, 0, W))
    near_key = jnp.where(holder == 0, local % NB, NB - 1 + near_code)

    far_rows = far_list[0].reshape(groups, FAR)
    mine = lax.dynamic_index_in_dim(far_rows, group, 0, keepdims=False)
    theirs = lax.dynamic_index_in_dim(far_rows, group ^ 1, 0, keepdims=False)
    far_code = place_of(mine // NB, chip, core, chips)
    needed = place_of(theirs // NB, chip, 1 - core, chips) == PICKED
    sent = jnp.where(needed, place_of(theirs // NB, chip, core, chips), PICKED)
    pick_table = jnp.stack([sent, theirs % NB]).astype(i32)

    self_code = jnp.zeros((NB, 1), i32)
    self_key = jnp.arange(NB, dtype=i32)[:, None]
    codes = jnp.concatenate([self_code, near_code, far_code.reshape(NB, EXP)], axis=1).reshape(-1)
    slots = jnp.concatenate([self_key, local % NB, (mine % NB).reshape(NB, EXP)], axis=1).reshape(-1)
    far_key = (NEAR + first_of(mine)).reshape(NB, EXP)
    targets = jnp.concatenate([self_key, near_key, far_key], axis=1).reshape(-1)
    leads = first_of(targets) == jnp.arange(ENTRIES, dtype=i32)
    table = jnp.stack([codes, slots, targets, leads.astype(i32)]).astype(i32)
    steps = [(4, 0), (3, 1), (3, 0), (2, 1), (2, 0), (1, 1), (1, 0)]
    direction = 1 - 2 * core
    wanted = []
    for distance, side in steps:
        cluster = ((chip + direction * distance) % chips) * 2 + jnp.where(side == 0, core, 1 - core)
        wanted += [cluster * NB, cluster * NB + 1]
    wanted += [group * NB, group * NB + 1]
    wanted = jnp.stack(wanted).astype(i32)
    hits = jnp.stack([slot_in(mine, wanted), slot_in(theirs, wanted)])
    last = jnp.concatenate([given, hits[1, 7 * NB :]]).astype(i32)
    tables = (given, pick_table, table, hits[:, : 2 * NB], hits[:, 2 * NB : 7 * NB], last)
    sibling, tables = lax.optimization_barrier((sibling, tables))
    given, pick_table, table, hits_first, hits_rest, last = tables

    flow_b = [ring_step(sibling)]
    flow_a.append(ring_step(flow_a[0]))
    keep, give = offer(given, keys, values)
    given_here = swap_cores(give)
    flow_b.append(ring_step(flow_b[0]))
    one = dom_step(jnp.stack([keep[0], given_here[0]]), 1)
    flow_a[1], one = lax.optimization_barrier((flow_a[1], one))
    flow_a.append(ring_step(flow_a[1]))
    keep, given_here, flow_b[1] = lax.optimization_barrier((keep, given_here, flow_b[1]))
    two = dom_step(jnp.stack([keep[1], given_here[1]]), 2)
    flow_b.append(ring_step(flow_b[1]))
    flow_a[2], two = lax.optimization_barrier((flow_a[2], two))
    flow_a.append(ring_step(flow_a[2]))
    near = (one, two, swap_cores(jnp.stack([one[1], two[1]])))

    picked = swap_cores(pick(pick_table, [sibling] + flow_a + flow_b))
    attended, grad_queries, own_terms, far_terms, keep, give = attend(
        table,
        queries.reshape(NB, BS, D),
        cotangent.reshape(NB, BS, D),
        own,
        near,
        [sibling] + flow_a + flow_b,
        picked,
    )

    sibling_terms = swap_cores(far_terms)
    start_a, start_b = spread(hits_first, far_terms, sibling_terms)
    a3, b2, a2, b1, a1 = spread(hits_rest, far_terms, sibling_terms)

    def joined(x, y):
        return (x.astype(F32) + y.astype(F32)).astype(BF)

    back_a = ring_step(start_a)
    back_b = ring_step(start_b)
    give, a3 = lax.optimization_barrier((give, a3))
    given_here = swap_cores(give)
    back_a = ring_step(joined(back_a, a3))
    back_b = ring_step(joined(back_b, b2))
    two = dom_step(jnp.stack([keep[1], given_here[1]]), -2)
    back_a, two = lax.optimization_barrier((back_a, two))
    back_a = ring_step(joined(back_a, a2))
    keep, given_here, back_b = lax.optimization_barrier((keep, given_here, back_b))
    one = dom_step(jnp.stack([keep[0], given_here[0]]), -1)
    back_b = ring_step(joined(back_b, b1))
    back_a, one = lax.optimization_barrier((back_a, one))
    back_a = ring_step(joined(back_a, a1))
    returned = (one, two, swap_cores(jnp.stack([one[1], two[1]])))
    back_b = swap_cores(back_b)

    grad_keys, grad_values = close(last, own_terms, sibling_terms, back_a, back_b, returned)
    return (attended.reshape(NB * BS, D), grad_queries.reshape(NB * BS, D), grad_keys, grad_values)


def solution(mesh):
    rows = P(("group", "dom"), None)
    return jax.shard_map(
        on_device,
        mesh=mesh,
        in_specs=(rows, rows, rows, rows, P("group", None), P("dom", None, None)),
        out_specs=(rows, rows, rows, rows),
        check_vma=False,
    )
```

```python
import functools
import math

import jax
import jax.numpy as jnp
from jax import lax
from jax.experimental import pallas as pl
from jax.experimental.pallas import tpu as pltpu
from jax.sharding import PartitionSpec as P

D = 512
BS = 128
NB = 2
LOC = 3
EXP = 3
W = 2
KB = 1 + LOC + EXP
ENTRIES = NB * KB
ROWS = KB * BS
FAR = NB * EXP
NEAR = NB + 2 * W
PAIRS = D // 128
BF = jnp.bfloat16
F32 = jnp.float32

HBM = pl.BlockSpec(memory_space=pltpu.HBM)
VMEM = pl.BlockSpec(memory_space=pltpu.VMEM)
SMEM = pl.BlockSpec(memory_space=pltpu.SMEM)

SIBLING, FLOW_A, FLOW_B, PICKED = 0, 0, 4, 8


def ring_step(array):
    size = lax.axis_size("group")
    return lax.ppermute(array, "group", [(g, (g + (2 if g % 2 == 0 else -2)) % size) for g in range(size)])


def swap_cores(array):
    size = lax.axis_size("group")
    return lax.ppermute(array, "group", [(g, g ^ 1) for g in range(size)])


def dom_step(array, by):
    groups, doms = lax.axis_size("group"), lax.axis_size("dom")
    pairs = []
    for g in range(groups):
        for i in range(doms):
            to = i + (by if g % 2 == 0 else -by)
            if 0 <= to < doms:
                pairs.append((g * doms + i, g * doms + to))
    return lax.ppermute(array, ("group", "dom"), pairs)


def place_of(cluster, chip, core, chips):
    other_chip, other_core = cluster // 2, cluster % 2
    distance = jnp.where(core == 0, chip - other_chip, other_chip - chip) % chips
    same = other_core == core
    half = chips // 2
    here = jnp.where(same, FLOW_A + distance, FLOW_B + distance)
    held = jnp.where(same, distance <= half, distance < half)
    return jnp.where(distance == 0, SIBLING, jnp.where(held, here, PICKED))


def first_of(values):
    order = jnp.arange(values.shape[0], dtype=jnp.int32)
    same = values[:, None] == values[None, :]
    return jnp.min(jnp.where(same, order[None, :], values.shape[0]), axis=1)


def slot_in(values, wanted):
    order = jnp.arange(values.shape[0], dtype=jnp.int32)
    hit = values[None, :] == wanted[:, None]
    found = jnp.min(jnp.where(hit, order[None, :], values.shape[0]), axis=1)
    return jnp.where(found == values.shape[0], -1, found).astype(jnp.int32)


def pick_kernel(table, *refs):
    places, out, sem = refs[:8], refs[8], refs[9]
    copies = []
    for t in range(FAR):
        for code, place in enumerate(places):

            @pl.when(table[0, t] == code)
            def _():
                rows = pl.ds(pl.multiple_of(table[1, t] * BS, BS), BS)
                pltpu.make_async_copy(place.at[:, rows, :], out.at[t], sem.at[t]).start()

    for t in range(FAR):

        @pl.when(table[0, t] < 8)
        def _():
            pltpu.make_async_copy(places[0].at[:, pl.ds(0, BS), :], out.at[t], sem.at[t]).wait()


def pick(table, places):
    return pl.pallas_call(
        pick_kernel,
        out_shape=jax.ShapeDtypeStruct((FAR, 2, BS, D), BF),
        in_specs=[SMEM] + [HBM] * 8,
        out_specs=VMEM,
        scratch_shapes=[pltpu.SemaphoreType.DMA((FAR,))],
        compiler_params=pltpu.CompilerParams(vmem_limit_bytes=4 * 2**20),
        cost_estimate=pl.CostEstimate(flops=0, bytes_accessed=6 * 2**20, transcendentals=0),
    )(table, *places)


def offer_kernel(table, keys, values, *refs):
    outs, sem = refs[:2], refs[2]
    copies = []
    for t in range(2 * W):
        rows = pl.ds(pl.multiple_of(table[t] * BS, BS), BS)
        for half, source in enumerate((keys, values)):
            target = outs[t // W].at[t % W, half]
            copies.append(pltpu.make_async_copy(source.at[rows, :], target, sem.at[t, half]))
    for copy in copies:
        copy.start()
    for copy in copies:
        copy.wait()


def offer(table, keys, values):
    return pl.pallas_call(
        offer_kernel,
        out_shape=(jax.ShapeDtypeStruct((W, 2, BS, D), BF),) * 2,
        in_specs=[SMEM, HBM, HBM],
        out_specs=(VMEM,) * 2,
        scratch_shapes=[pltpu.SemaphoreType.DMA((2 * W, 2))],
        compiler_params=pltpu.CompilerParams(vmem_limit_bytes=4 * 2**20),
        cost_estimate=pl.CostEstimate(flops=0, bytes_accessed=2 * 2**20, transcendentals=0),
    )(table, keys, values)


def attend_pair(step, table, q_ref, g_ref, listed, att_ref, gq_ref, totals):
    low = lax.broadcasted_iota(jnp.int32, (BS, 128), 1) < 64
    last = (((1,), (1,)), ((), ()))
    first = (((0,), (0,)), ((), ()))
    s = step // PAIRS
    p = step % PAIRS
    cols = pl.ds(pl.multiple_of(p * 128, 128), 128)
    query = q_ref[s, :, cols]
    grad = g_ref[s, :, cols]
    zero = jnp.zeros_like(query)
    query2 = jnp.concatenate([jnp.where(low, query, zero), jnp.where(low, zero, query)], axis=0)
    grad2 = jnp.concatenate([jnp.where(low, grad, zero), jnp.where(low, zero, grad)], axis=0)
    keys = listed[s, 0, :, cols]
    values = listed[s, 1, :, cols]

    def own_heads(both):
        return jnp.concatenate([both[:64, :128], both[64:, 128:]], axis=0)

    scores = lax.dot_general(keys, query2, last, preferred_element_type=F32)
    highest = jnp.max(scores, axis=0, keepdims=True)
    raised = jnp.exp2((scores - highest) * (0.125 * math.log2(math.e)))
    weights = raised * (1.0 / jnp.sum(raised, axis=0, keepdims=True))
    weights_low = weights.astype(BF)
    mixture = own_heads(lax.dot_general(values, weights_low, first, preferred_element_type=F32))
    att_ref[s, :, cols] = mixture.T.astype(BF)
    product = mixture * grad.astype(F32).T
    carried = jnp.concatenate(
        [jnp.sum(product[:64], axis=0, keepdims=True), jnp.sum(product[64:], axis=0, keepdims=True)], axis=1
    )
    grad_weights = lax.dot_general(values, grad2, last, preferred_element_type=F32)
    grad_scores = ((weights * (grad_weights - carried)) * 0.125).astype(BF)
    grad_query = own_heads(lax.dot_general(keys, grad_scores, first, preferred_element_type=F32))
    gq_ref[s, :, cols] = grad_query.T.astype(BF)
    grad_key = jnp.dot(grad_scores, query2, preferred_element_type=F32)
    grad_value = jnp.dot(weights_low, grad2, preferred_element_type=F32)
    for j in range(KB):
        slot = table[2, s * KB + j]
        again = table[3, s * KB + j] == 0
        rows = slice(j * BS, (j + 1) * BS)
        for half, term in enumerate((grad_key, grad_value)):
            before = totals[slot, half, :, cols]
            totals[slot, half, :, cols] = jnp.where(again, before, 0.0) + term[rows]


def attend_kernel(table, q_ref, g_ref, *refs):
    own, (one, two, other), places, picked = refs[0], refs[1:4], refs[4:12], refs[12]
    near = (one.at[0], two.at[0], other.at[0], other.at[1])
    att_ref, gq_ref, own_out, far_out, keep_out, give_out, listed, totals, sem = refs[13:]

    def bring(source, s, j):
        pltpu.make_async_copy(source, listed.at[s, :, pl.ds(j * BS, BS), :], sem.at[s]).start()

    for s in range(NB):
        bring(own.at[:, pl.ds(s * BS, BS), :], s, 0)
        for j in range(1, KB):
            code, place = table[0, s * KB + j], table[1, s * KB + j]
            rows = pl.ds(pl.multiple_of(place * BS, BS), BS)
            if j <= LOC:

                @pl.when(code == 0)
                def _():
                    bring(own.at[:, rows, :], s, j)

                for t in range(2 * W):

                    @pl.when(code == 1 + t)
                    def _():
                        bring(near[t], s, j)

            else:
                for t in range(8):

                    @pl.when(code == t)
                    def _():
                        bring(places[t].at[:, rows, :], s, j)

                @pl.when(code == 8)
                def _():
                    bring(picked.at[s * EXP + j - 1 - LOC], s, j)

    def body(step, carry):
        attend_pair(step, table, q_ref, g_ref, listed, att_ref, gq_ref, totals)
        return carry

    for s in range(NB):
        pltpu.make_async_copy(listed.at[s], listed.at[s], sem.at[s]).wait()
        lax.fori_loop(s * PAIRS, (s + 1) * PAIRS, body, 0, unroll=PAIRS)
    own_out[...] = totals[:NB].astype(BF)
    keep_out[...] = totals[NB : NB + W].astype(BF)
    give_out[...] = totals[NB + W : NEAR].astype(BF)
    far_out[...] = totals[NEAR:].astype(BF)


def attend(table, queries, cotangent, own, near, places, picked):
    return pl.pallas_call(
        attend_kernel,
        out_shape=(
            jax.ShapeDtypeStruct((NB, BS, D), BF),
            jax.ShapeDtypeStruct((NB, BS, D), BF),
            jax.ShapeDtypeStruct((NB, 2, BS, D), BF),
            jax.ShapeDtypeStruct((FAR, 2, BS, D), BF),
        )
        + (jax.ShapeDtypeStruct((W, 2, BS, D), BF),) * 2,
        in_specs=[SMEM, VMEM, VMEM] + [HBM] * 13,
        out_specs=(VMEM,) * 6,
        scratch_shapes=[
            pltpu.VMEM((NB, 2, ROWS, D), BF),
            pltpu.VMEM((NEAR + FAR, 2, BS, D), F32),
            pltpu.SemaphoreType.DMA((NB,)),
        ],
        compiler_params=pltpu.CompilerParams(vmem_limit_bytes=32 * 2**20),
        cost_estimate=pl.CostEstimate(
            flops=12 * NB * BS * ROWS * D, bytes_accessed=12 * 2**20, transcendentals=NB * 8 * BS * ROWS
        ),
    )(table, queries, cotangent, own, *near, *places, picked)


def spread_kernel(count, table, mine, theirs, *outs):
    for n in range(count):
        out = outs[n]
        for s in range(NB):
            a, b = table[0, n * NB + s], table[1, n * NB + s]

            @pl.when((a < 0) & (b < 0))
            def _():
                out[s] = jnp.zeros((2, BS, D), BF)

            @pl.when((a >= 0) & (b < 0))
            def _():
                out[s] = mine[a]

            @pl.when((a < 0) & (b >= 0))
            def _():
                out[s] = theirs[b]

            @pl.when((a >= 0) & (b >= 0))
            def _():
                out[s] = (mine[a].astype(F32) + theirs[b].astype(F32)).astype(BF)


def spread(table, mine, theirs):
    count = table.shape[1] // NB
    return pl.pallas_call(
        functools.partial(spread_kernel, count),
        out_shape=tuple(jax.ShapeDtypeStruct((NB, 2, BS, D), BF) for _ in range(count)),
        in_specs=[SMEM, VMEM, VMEM],
        out_specs=(VMEM,) * count,
        compiler_params=pltpu.CompilerParams(vmem_limit_bytes=12 * 2**20),
        cost_estimate=pl.CostEstimate(flops=0, bytes_accessed=(3 + count) * 2**19, transcendentals=0),
    )(table, mine, theirs)


def close_kernel(table, near, theirs, from_a, from_b, *refs):
    (one, two, other), (gk_ref, gv_ref) = refs[:3], refs[3:]
    returned = (one.at[0], two.at[0], other.at[0], other.at[1])
    for s in range(NB):
        for half, out in enumerate((gk_ref, gv_ref)):
            total = near[s, half].astype(F32)
            for t in range(2 * W):
                total = total + jnp.where(table[t] == s, returned[t][half].astype(F32), 0.0)
            total = total + from_a[s, half].astype(F32) + from_b[s, half].astype(F32)
            b = table[4 + s]
            direct = theirs[jnp.maximum(b, 0), half].astype(F32)
            total = total + jnp.where(b >= 0, direct, 0.0)
            out[pl.ds(s * BS, BS), :] = total.astype(BF)


def close(table, near, theirs, from_a, from_b, returned):
    return pl.pallas_call(
        close_kernel,
        out_shape=(jax.ShapeDtypeStruct((NB * BS, D), BF),) * 2,
        in_specs=[SMEM] + [VMEM] * 7,
        out_specs=(VMEM, VMEM),
        compiler_params=pltpu.CompilerParams(vmem_limit_bytes=12 * 2**20),
        cost_estimate=pl.CostEstimate(flops=2**22, bytes_accessed=6 * 2**20, transcendentals=0),
    )(table, near, theirs, from_a, from_b, *returned)


def on_device(queries, keys, values, cotangent, local_list, far_list):
    groups = lax.axis_size("group")
    doms = lax.axis_size("dom")
    chips = groups // 2
    dom = lax.axis_index("dom").astype(jnp.int32)
    group = lax.axis_index("group").astype(jnp.int32)
    chip, core = group // 2, group % 2
    i32 = jnp.int32

    own = jnp.stack([keys, values])
    flow_a = [ring_step(own)]
    sibling = swap_cores(own)

    padded = jnp.pad(local_list, ((W * NB, W * NB), (0, 0)), constant_values=-1)
    around = lax.dynamic_slice_in_dim(padded, dom * NB, (2 * W + 1) * NB, 0).reshape(2 * W + 1, NB * LOC)
    given = jnp.max(jnp.where(around // NB == dom, around % NB, 0), axis=1).astype(i32)
    up, down = given[W + 1 :], given[:W][::-1]
    given = jnp.where(core == 0, jnp.concatenate([up, down]), jnp.concatenate([down, up]))
    local = around[W].reshape(NB, LOC)
    holder = local // NB - dom
    direct = (holder < 0) == (core == 0)
    near_code = jnp.where(holder == 0, 0, jnp.abs(holder) + jnp.where(direct, 0, W))
    near_key = jnp.where(holder == 0, local % NB, NB - 1 + near_code)

    far_rows = far_list[0].reshape(groups, FAR)
    mine = lax.dynamic_index_in_dim(far_rows, group, 0, keepdims=False)
    theirs = lax.dynamic_index_in_dim(far_rows, group ^ 1, 0, keepdims=False)
    far_code = place_of(mine // NB, chip, core, chips)
    needed = place_of(theirs // NB, chip, 1 - core, chips) == PICKED
    sent = jnp.where(needed, place_of(theirs // NB, chip, core, chips), PICKED)
    pick_table = jnp.stack([sent, theirs % NB]).astype(i32)

    self_code = jnp.zeros((NB, 1), i32)
    self_key = jnp.arange(NB, dtype=i32)[:, None]
    codes = jnp.concatenate([self_code, near_code, far_code.reshape(NB, EXP)], axis=1).reshape(-1)
    slots = jnp.concatenate([self_key, local % NB, (mine % NB).reshape(NB, EXP)], axis=1).reshape(-1)
    far_key = (NEAR + first_of(mine)).reshape(NB, EXP)
    targets = jnp.concatenate([self_key, near_key, far_key], axis=1).reshape(-1)
    leads = first_of(targets) == jnp.arange(ENTRIES, dtype=i32)
    table = jnp.stack([codes, slots, targets, leads.astype(i32)]).astype(i32)
    steps = [(4, 0), (3, 1), (3, 0), (2, 1), (2, 0), (1, 1), (1, 0)]
    direction = 1 - 2 * core
    wanted = []
    for distance, side in steps:
        cluster = ((chip + direction * distance) % chips) * 2 + jnp.where(side == 0, core, 1 - core)
        wanted += [cluster * NB, cluster * NB + 1]
    wanted += [group * NB, group * NB + 1]
    wanted = jnp.stack(wanted).astype(i32)
    hits = jnp.stack([slot_in(mine, wanted), slot_in(theirs, wanted)])
    last = jnp.concatenate([given, hits[1, 7 * NB :]]).astype(i32)
    tables = (given, pick_table, table, hits[:, : 2 * NB], hits[:, 2 * NB : 7 * NB], last)
    sibling, tables = lax.optimization_barrier((sibling, tables))
    given, pick_table, table, hits_first, hits_rest, last = tables

    flow_b = [ring_step(sibling)]
    flow_a.append(ring_step(flow_a[0]))
    keep, give = offer(given, keys, values)
    given_here = swap_cores(give)
    flow_b.append(ring_step(flow_b[0]))
    two = dom_step(jnp.stack([keep[1], given_here[1]]), 2)
    flow_a.append(ring_step(flow_a[1]))
    flow_b[1], two = lax.optimization_barrier((flow_b[1], two))
    flow_b.append(ring_step(flow_b[1]))
    keep, given_here, two = lax.optimization_barrier((keep, given_here, two))
    one = dom_step(jnp.stack([keep[0], given_here[0]]), 1)
    flow_a.append(ring_step(flow_a[2]))
    flow_a[3], one = lax.optimization_barrier((flow_a[3], one))
    near = (one, two, swap_cores(jnp.stack([one[1], two[1]])))

    picked = swap_cores(pick(pick_table, [sibling] + flow_a + flow_b))
    attended, grad_queries, own_terms, far_terms, keep, give = attend(
        table,
        queries.reshape(NB, BS, D),
        cotangent.reshape(NB, BS, D),
        own,
        near,
        [sibling] + flow_a + flow_b,
        picked,
    )

    sibling_terms = swap_cores(far_terms)
    sibling_terms, give = lax.optimization_barrier((sibling_terms, give))
    start_a, start_b = spread(hits_first, far_terms, sibling_terms)
    a3, b2, a2, b1, a1 = spread(hits_rest, far_terms, sibling_terms)

    def joined(x, y):
        return (x.astype(F32) + y.astype(F32)).astype(BF)

    back_a = ring_step(start_a)
    back_b = ring_step(start_b)
    given_here = swap_cores(give)
    back_a = ring_step(joined(back_a, a3))
    two = dom_step(jnp.stack([keep[1], given_here[1]]), -2)
    back_b = ring_step(joined(back_b, b2))
    back_a = ring_step(joined(back_a, a2))
    back_b, two = lax.optimization_barrier((back_b, two))
    back_b = ring_step(joined(back_b, b1))
    keep, given_here, two = lax.optimization_barrier((keep, given_here, two))
    one = dom_step(jnp.stack([keep[0], given_here[0]]), -1)
    back_a = ring_step(joined(back_a, a1))
    other, back_b = lax.optimization_barrier((jnp.stack([one[1], two[1]]), back_b))
    back_b = swap_cores(back_b)
    returned = (one, two, swap_cores(other))

    grad_keys, grad_values = close(last, own_terms, sibling_terms, back_a, back_b, returned)
    return (attended.reshape(NB * BS, D), grad_queries.reshape(NB * BS, D), grad_keys, grad_values)


def solution(mesh):
    rows = P(("group", "dom"), None)
    return jax.shard_map(
        on_device,
        mesh=mesh,
        in_specs=(rows, rows, rows, rows, P("group", None), P("dom", None, None)),
        out_specs=(rows, rows, rows, rows),
        check_vma=False,
    )
```

```python
import functools
import math

import jax
import jax.numpy as jnp
from jax import lax
from jax.experimental import pallas as pl
from jax.experimental.pallas import tpu as pltpu
from jax.sharding import PartitionSpec as P

D = 512
BS = 128
NB = 2
LOC = 3
EXP = 3
W = 2
KB = 1 + LOC + EXP
ENTRIES = NB * KB
ROWS = KB * BS
FAR = NB * EXP
NEAR = NB + 2 * W
PAIRS = D // 128
BF = jnp.bfloat16
F32 = jnp.float32

HBM = pl.BlockSpec(memory_space=pltpu.HBM)
VMEM = pl.BlockSpec(memory_space=pltpu.VMEM)
SMEM = pl.BlockSpec(memory_space=pltpu.SMEM)

SIBLING, FLOW_A, FLOW_B, PICKED = 0, 0, 4, 8


def ring_step(array):
    size = lax.axis_size("group")
    return lax.ppermute(array, "group", [(g, (g + (2 if g % 2 == 0 else -2)) % size) for g in range(size)])


def swap_cores(array):
    size = lax.axis_size("group")
    return lax.ppermute(array, "group", [(g, g ^ 1) for g in range(size)])


def dom_step(array, by):
    groups, doms = lax.axis_size("group"), lax.axis_size("dom")
    pairs = []
    for g in range(groups):
        for i in range(doms):
            to = i + (by if g % 2 == 0 else -by)
            if 0 <= to < doms:
                pairs.append((g * doms + i, g * doms + to))
    return lax.ppermute(array, ("group", "dom"), pairs)


def place_of(cluster, chip, core, chips):
    other_chip, other_core = cluster // 2, cluster % 2
    distance = jnp.where(core == 0, chip - other_chip, other_chip - chip) % chips
    same = other_core == core
    half = chips // 2
    here = jnp.where(same, FLOW_A + distance, FLOW_B + distance)
    held = jnp.where(same, distance <= half, distance < half)
    return jnp.where(distance == 0, SIBLING, jnp.where(held, here, PICKED))


def first_of(values):
    order = jnp.arange(values.shape[0], dtype=jnp.int32)
    same = values[:, None] == values[None, :]
    return jnp.min(jnp.where(same, order[None, :], values.shape[0]), axis=1)


def slot_in(values, wanted):
    order = jnp.arange(values.shape[0], dtype=jnp.int32)
    hit = values[None, :] == wanted[:, None]
    found = jnp.min(jnp.where(hit, order[None, :], values.shape[0]), axis=1)
    return jnp.where(found == values.shape[0], -1, found).astype(jnp.int32)


def pick_kernel(table, *refs):
    places, out, sem = refs[:8], refs[8], refs[9]
    copies = []
    for t in range(FAR):
        for code, place in enumerate(places):

            @pl.when(table[0, t] == code)
            def _():
                rows = pl.ds(pl.multiple_of(table[1, t] * BS, BS), BS)
                pltpu.make_async_copy(place.at[:, rows, :], out.at[t], sem.at[t]).start()

    for t in range(FAR):

        @pl.when(table[0, t] < 8)
        def _():
            pltpu.make_async_copy(places[0].at[:, pl.ds(0, BS), :], out.at[t], sem.at[t]).wait()


def pick(table, places):
    return pl.pallas_call(
        pick_kernel,
        out_shape=jax.ShapeDtypeStruct((FAR, 2, BS, D), BF),
        in_specs=[SMEM] + [HBM] * 8,
        out_specs=VMEM,
        scratch_shapes=[pltpu.SemaphoreType.DMA((FAR,))],
        compiler_params=pltpu.CompilerParams(vmem_limit_bytes=4 * 2**20),
        cost_estimate=pl.CostEstimate(flops=0, bytes_accessed=6 * 2**20, transcendentals=0),
    )(table, *places)


def offer_kernel(table, keys, values, *refs):
    outs, sem = refs[:2], refs[2]
    copies = []
    for t in range(2 * W):
        rows = pl.ds(pl.multiple_of(table[t] * BS, BS), BS)
        for half, source in enumerate((keys, values)):
            target = outs[t // W].at[t % W, half]
            copies.append(pltpu.make_async_copy(source.at[rows, :], target, sem.at[t, half]))
    for copy in copies:
        copy.start()
    for copy in copies:
        copy.wait()


def offer(table, keys, values):
    return pl.pallas_call(
        offer_kernel,
        out_shape=(jax.ShapeDtypeStruct((W, 2, BS, D), BF),) * 2,
        in_specs=[SMEM, HBM, HBM],
        out_specs=(VMEM,) * 2,
        scratch_shapes=[pltpu.SemaphoreType.DMA((2 * W, 2))],
        compiler_params=pltpu.CompilerParams(vmem_limit_bytes=4 * 2**20),
        cost_estimate=pl.CostEstimate(flops=0, bytes_accessed=2 * 2**20, transcendentals=0),
    )(table, keys, values)


def attend_pair(step, table, q_ref, g_ref, listed, att_ref, gq_ref, totals):
    low = lax.broadcasted_iota(jnp.int32, (BS, 128), 1) < 64
    last = (((1,), (1,)), ((), ()))
    first = (((0,), (0,)), ((), ()))
    s = step // PAIRS
    p = step % PAIRS
    cols = pl.ds(pl.multiple_of(p * 128, 128), 128)
    query = q_ref[s, :, cols]
    grad = g_ref[s, :, cols]
    zero = jnp.zeros_like(query)
    query2 = jnp.concatenate([jnp.where(low, query, zero), jnp.where(low, zero, query)], axis=0)
    grad2 = jnp.concatenate([jnp.where(low, grad, zero), jnp.where(low, zero, grad)], axis=0)
    keys = listed[s, 0, :, cols]
    values = listed[s, 1, :, cols]

    def own_heads(both):
        return jnp.concatenate([both[:64, :128], both[64:, 128:]], axis=0)

    scores = lax.dot_general(keys, query2, last, preferred_element_type=F32)
    grad_weights = lax.dot_general(values, grad2, last, preferred_element_type=F32)
    highest = jnp.max(scores, axis=0, keepdims=True)
    raised = jnp.exp2((scores - highest) * (0.125 * math.log2(math.e)))
    weights = raised * (1.0 / jnp.sum(raised, axis=0, keepdims=True))
    weights_low = weights.astype(BF)
    grad_value = jnp.dot(weights_low, grad2, preferred_element_type=F32)
    mixture = own_heads(lax.dot_general(values, weights_low, first, preferred_element_type=F32))
    att_ref[s, :, cols] = mixture.T.astype(BF)
    product = mixture * grad.astype(F32).T
    carried = jnp.concatenate(
        [jnp.sum(product[:64], axis=0, keepdims=True), jnp.sum(product[64:], axis=0, keepdims=True)], axis=1
    )
    grad_scores = ((weights * (grad_weights - carried)) * 0.125).astype(BF)
    grad_query = own_heads(lax.dot_general(keys, grad_scores, first, preferred_element_type=F32))
    gq_ref[s, :, cols] = grad_query.T.astype(BF)
    grad_key = jnp.dot(grad_scores, query2, preferred_element_type=F32)
    for j in range(KB):
        slot = table[2, s * KB + j]
        again = table[3, s * KB + j] == 0
        rows = slice(j * BS, (j + 1) * BS)
        for half, term in enumerate((grad_key, grad_value)):
            before = totals[slot, half, :, cols]
            totals[slot, half, :, cols] = jnp.where(again, before, 0.0) + term[rows]


def attend_kernel(table, q_ref, g_ref, *refs):
    own, (one, two, other), places, picked = refs[0], refs[1:4], refs[4:12], refs[12]
    near = (one.at[0], two.at[0], other.at[0], other.at[1])
    att_ref, gq_ref, own_out, far_out, keep_out, give_out, listed, totals, sem = refs[13:]

    def bring(source, s, j):
        pltpu.make_async_copy(source, listed.at[s, :, pl.ds(j * BS, BS), :], sem.at[s]).start()

    for s in range(NB):
        bring(own.at[:, pl.ds(s * BS, BS), :], s, 0)
        for j in range(1, KB):
            code, place = table[0, s * KB + j], table[1, s * KB + j]
            rows = pl.ds(pl.multiple_of(place * BS, BS), BS)
            if j <= LOC:

                @pl.when(code == 0)
                def _():
                    bring(own.at[:, rows, :], s, j)

                for t in range(2 * W):

                    @pl.when(code == 1 + t)
                    def _():
                        bring(near[t], s, j)

            else:
                for t in range(8):

                    @pl.when(code == t)
                    def _():
                        bring(places[t].at[:, rows, :], s, j)

                @pl.when(code == 8)
                def _():
                    bring(picked.at[s * EXP + j - 1 - LOC], s, j)

    def body(step, carry):
        attend_pair(step, table, q_ref, g_ref, listed, att_ref, gq_ref, totals)
        return carry

    for s in range(NB):
        pltpu.make_async_copy(listed.at[s], listed.at[s], sem.at[s]).wait()

    def body(step, carry):
        attend_pair(step, table, q_ref, g_ref, listed, att_ref, gq_ref, totals)
        return carry

    lax.fori_loop(0, NB * PAIRS, body, 0, unroll=PAIRS)
    own_out[...] = totals[:NB].astype(BF)
    keep_out[...] = totals[NB : NB + W].astype(BF)
    give_out[...] = totals[NB + W : NEAR].astype(BF)
    far_out[...] = totals[NEAR:].astype(BF)


def attend(table, queries, cotangent, own, near, places, picked):
    return pl.pallas_call(
        attend_kernel,
        out_shape=(
            jax.ShapeDtypeStruct((NB, BS, D), BF),
            jax.ShapeDtypeStruct((NB, BS, D), BF),
            jax.ShapeDtypeStruct((NB, 2, BS, D), BF),
            jax.ShapeDtypeStruct((FAR, 2, BS, D), BF),
        )
        + (jax.ShapeDtypeStruct((W, 2, BS, D), BF),) * 2,
        in_specs=[SMEM, VMEM, VMEM] + [HBM] * 13,
        out_specs=(VMEM,) * 6,
        scratch_shapes=[
            pltpu.VMEM((NB, 2, ROWS, D), BF),
            pltpu.VMEM((NEAR + FAR, 2, BS, D), F32),
            pltpu.SemaphoreType.DMA((NB,)),
        ],
        compiler_params=pltpu.CompilerParams(vmem_limit_bytes=32 * 2**20),
        cost_estimate=pl.CostEstimate(
            flops=12 * NB * BS * ROWS * D, bytes_accessed=12 * 2**20, transcendentals=NB * 8 * BS * ROWS
        ),
    )(table, queries, cotangent, own, *near, *places, picked)


def spread_kernel(count, table, mine, theirs, *outs):
    for n in range(count):
        out = outs[n]
        for s in range(NB):
            a, b = table[0, n * NB + s], table[1, n * NB + s]

            @pl.when((a < 0) & (b < 0))
            def _():
                out[s] = jnp.zeros((2, BS, D), BF)

            @pl.when((a >= 0) & (b < 0))
            def _():
                out[s] = mine[a]

            @pl.when((a < 0) & (b >= 0))
            def _():
                out[s] = theirs[b]

            @pl.when((a >= 0) & (b >= 0))
            def _():
                out[s] = (mine[a].astype(F32) + theirs[b].astype(F32)).astype(BF)


def spread(table, mine, theirs):
    count = table.shape[1] // NB
    return pl.pallas_call(
        functools.partial(spread_kernel, count),
        out_shape=tuple(jax.ShapeDtypeStruct((NB, 2, BS, D), BF) for _ in range(count)),
        in_specs=[SMEM, VMEM, VMEM],
        out_specs=(VMEM,) * count,
        compiler_params=pltpu.CompilerParams(vmem_limit_bytes=12 * 2**20),
        cost_estimate=pl.CostEstimate(flops=0, bytes_accessed=(3 + count) * 2**19, transcendentals=0),
    )(table, mine, theirs)


def close_kernel(table, near, theirs, from_a, from_b, *refs):
    (one, two, other), (gk_ref, gv_ref) = refs[:3], refs[3:]
    returned = (one.at[0], two.at[0], other.at[0], other.at[1])
    for s in range(NB):
        for half, out in enumerate((gk_ref, gv_ref)):
            total = near[s, half].astype(F32)
            for t in range(2 * W):
                total = total + jnp.where(table[t] == s, returned[t][half].astype(F32), 0.0)
            total = total + from_a[s, half].astype(F32) + from_b[s, half].astype(F32)
            b = table[4 + s]
            direct = theirs[jnp.maximum(b, 0), half].astype(F32)
            total = total + jnp.where(b >= 0, direct, 0.0)
            out[pl.ds(s * BS, BS), :] = total.astype(BF)


def close(table, near, theirs, from_a, from_b, returned):
    return pl.pallas_call(
        close_kernel,
        out_shape=(jax.ShapeDtypeStruct((NB * BS, D), BF),) * 2,
        in_specs=[SMEM] + [VMEM] * 7,
        out_specs=(VMEM, VMEM),
        compiler_params=pltpu.CompilerParams(vmem_limit_bytes=12 * 2**20),
        cost_estimate=pl.CostEstimate(flops=2**22, bytes_accessed=6 * 2**20, transcendentals=0),
    )(table, near, theirs, from_a, from_b, *returned)


def on_device(queries, keys, values, cotangent, local_list, far_list):
    groups = lax.axis_size("group")
    doms = lax.axis_size("dom")
    chips = groups // 2
    dom = lax.axis_index("dom").astype(jnp.int32)
    group = lax.axis_index("group").astype(jnp.int32)
    chip, core = group // 2, group % 2
    i32 = jnp.int32

    own = jnp.stack([keys, values])
    flow_a = [ring_step(own)]
    sibling = swap_cores(own)

    padded = jnp.pad(local_list, ((W * NB, W * NB), (0, 0)), constant_values=-1)
    around = lax.dynamic_slice_in_dim(padded, dom * NB, (2 * W + 1) * NB, 0).reshape(2 * W + 1, NB * LOC)
    given = jnp.max(jnp.where(around // NB == dom, around % NB, 0), axis=1).astype(i32)
    up, down = given[W + 1 :], given[:W][::-1]
    given = jnp.where(core == 0, jnp.concatenate([up, down]), jnp.concatenate([down, up]))
    local = around[W].reshape(NB, LOC)
    holder = local // NB - dom
    direct = (holder < 0) == (core == 0)
    near_code = jnp.where(holder == 0, 0, jnp.abs(holder) + jnp.where(direct, 0, W))
    near_key = jnp.where(holder == 0, local % NB, NB - 1 + near_code)

    far_rows = far_list[0].reshape(groups, FAR)
    mine = lax.dynamic_index_in_dim(far_rows, group, 0, keepdims=False)
    theirs = lax.dynamic_index_in_dim(far_rows, group ^ 1, 0, keepdims=False)
    far_code = place_of(mine // NB, chip, core, chips)
    needed = place_of(theirs // NB, chip, 1 - core, chips) == PICKED
    sent = jnp.where(needed, place_of(theirs // NB, chip, core, chips), PICKED)
    pick_table = jnp.stack([sent, theirs % NB]).astype(i32)

    self_code = jnp.zeros((NB, 1), i32)
    self_key = jnp.arange(NB, dtype=i32)[:, None]
    codes = jnp.concatenate([self_code, near_code, far_code.reshape(NB, EXP)], axis=1).reshape(-1)
    slots = jnp.concatenate([self_key, local % NB, (mine % NB).reshape(NB, EXP)], axis=1).reshape(-1)
    far_key = (NEAR + first_of(mine)).reshape(NB, EXP)
    targets = jnp.concatenate([self_key, near_key, far_key], axis=1).reshape(-1)
    leads = first_of(targets) == jnp.arange(ENTRIES, dtype=i32)
    table = jnp.stack([codes, slots, targets, leads.astype(i32)]).astype(i32)
    steps = [(4, 0), (3, 1), (3, 0), (2, 1), (2, 0), (1, 1), (1, 0)]
    direction = 1 - 2 * core
    wanted = []
    for distance, side in steps:
        cluster = ((chip + direction * distance) % chips) * 2 + jnp.where(side == 0, core, 1 - core)
        wanted += [cluster * NB, cluster * NB + 1]
    wanted += [group * NB, group * NB + 1]
    wanted = jnp.stack(wanted).astype(i32)
    hits = jnp.stack([slot_in(mine, wanted), slot_in(theirs, wanted)])
    last = jnp.concatenate([given, hits[1, 7 * NB :]]).astype(i32)
    tables = (given, pick_table, table, hits[:, : 2 * NB], hits[:, 2 * NB : 7 * NB], last)
    sibling, tables = lax.optimization_barrier((sibling, tables))
    flow_b = [ring_step(sibling)]
    given, pick_table, table, hits_first, hits_rest, last = tables

    flow_a.append(ring_step(flow_a[0]))
    keep, give = offer(given, keys, values)
    given_here = swap_cores(give)
    flow_b.append(ring_step(flow_b[0]))
    two = dom_step(jnp.stack([keep[1], given_here[1]]), 2)
    flow_a.append(ring_step(flow_a[1]))
    flow_b[1], two = lax.optimization_barrier((flow_b[1], two))
    flow_b.append(ring_step(flow_b[1]))
    keep, given_here, two = lax.optimization_barrier((keep, given_here, two))
    one = dom_step(jnp.stack([keep[0], given_here[0]]), 1)
    flow_a.append(ring_step(flow_a[2]))
    flow_a[3], one = lax.optimization_barrier((flow_a[3], one))
    near = (one, two, swap_cores(jnp.stack([one[1], two[1]])))

    picked = swap_cores(pick(pick_table, [sibling] + flow_a + flow_b))
    attended, grad_queries, own_terms, far_terms, keep, give = attend(
        table,
        queries.reshape(NB, BS, D),
        cotangent.reshape(NB, BS, D),
        own,
        near,
        [sibling] + flow_a + flow_b,
        picked,
    )

    sibling_terms = swap_cores(far_terms)
    sibling_terms, give = lax.optimization_barrier((sibling_terms, give))
    start_a, start_b = spread(hits_first, far_terms, sibling_terms)
    a3, b2, a2, b1, a1 = spread(hits_rest, far_terms, sibling_terms)

    def joined(x, y):
        return (x.astype(F32) + y.astype(F32)).astype(BF)

    back_a = ring_step(start_a)
    back_b = ring_step(start_b)
    given_here = swap_cores(give)
    back_a = ring_step(joined(back_a, a3))
    two = dom_step(jnp.stack([keep[1], given_here[1]]), -2)
    back_b = ring_step(joined(back_b, b2))
    back_a = ring_step(joined(back_a, a2))
    back_b, two = lax.optimization_barrier((back_b, two))
    back_b = ring_step(joined(back_b, b1))
    keep, given_here, two = lax.optimization_barrier((keep, given_here, two))
    one = dom_step(jnp.stack([keep[0], given_here[0]]), -1)
    back_a = ring_step(joined(back_a, a1))
    other, back_b = lax.optimization_barrier((jnp.stack([one[1], two[1]]), back_b))
    back_b = swap_cores(back_b)
    returned = (one, two, swap_cores(other))

    grad_keys, grad_values = close(last, own_terms, sibling_terms, back_a, back_b, returned)
    return (attended.reshape(NB * BS, D), grad_queries.reshape(NB * BS, D), grad_keys, grad_values)


def solution(mesh):
    rows = P(("group", "dom"), None)
    return jax.shard_map(
        on_device,
        mesh=mesh,
        in_specs=(rows, rows, rows, rows, P("group", None), P("dom", None, None)),
        out_specs=(rows, rows, rows, rows),
        check_vma=False,
    )
```

```python
import functools
import math

import jax
import jax.numpy as jnp
from jax import lax
from jax.experimental import pallas as pl
from jax.experimental.pallas import tpu as pltpu
from jax.sharding import PartitionSpec as P

D = 512
BS = 128
NB = 2
LOC = 3
EXP = 3
W = 2
KB = 1 + LOC + EXP
ENTRIES = NB * KB
ROWS = KB * BS
FAR = NB * EXP
NEAR = NB + 2 * W
PAIRS = D // 128
BF = jnp.bfloat16
F32 = jnp.float32

HBM = pl.BlockSpec(memory_space=pltpu.HBM)
VMEM = pl.BlockSpec(memory_space=pltpu.VMEM)
SMEM = pl.BlockSpec(memory_space=pltpu.SMEM)

SIBLING, FLOW_A, FLOW_B, PICKED = 0, 0, 4, 8


def ring_step(array):
    size = lax.axis_size("group")
    return lax.ppermute(array, "group", [(g, (g + (2 if g % 2 == 0 else -2)) % size) for g in range(size)])


def swap_cores(array):
    size = lax.axis_size("group")
    return lax.ppermute(array, "group", [(g, g ^ 1) for g in range(size)])


def dom_step(array, by):
    groups, doms = lax.axis_size("group"), lax.axis_size("dom")
    pairs = []
    for g in range(groups):
        for i in range(doms):
            to = i + (by if g % 2 == 0 else -by)
            if 0 <= to < doms:
                pairs.append((g * doms + i, g * doms + to))
    return lax.ppermute(array, ("group", "dom"), pairs)


def place_of(cluster, chip, core, chips):
    other_chip, other_core = cluster // 2, cluster % 2
    distance = jnp.where(core == 0, chip - other_chip, other_chip - chip) % chips
    same = other_core == core
    half = chips // 2
    here = jnp.where(same, FLOW_A + distance, FLOW_B + distance)
    held = jnp.where(same, distance <= half, distance < half)
    return jnp.where(distance == 0, SIBLING, jnp.where(held, here, PICKED))


def first_of(values):
    order = jnp.arange(values.shape[0], dtype=jnp.int32)
    same = values[:, None] == values[None, :]
    return jnp.min(jnp.where(same, order[None, :], values.shape[0]), axis=1)


def slot_in(values, wanted):
    order = jnp.arange(values.shape[0], dtype=jnp.int32)
    hit = values[None, :] == wanted[:, None]
    found = jnp.min(jnp.where(hit, order[None, :], values.shape[0]), axis=1)
    return jnp.where(found == values.shape[0], -1, found).astype(jnp.int32)


def pick_kernel(table, *refs):
    places, out, sem = refs[:8], refs[8], refs[9]
    copies = []
    for t in range(FAR):
        for code, place in enumerate(places):

            @pl.when(table[0, t] == code)
            def _():
                rows = pl.ds(pl.multiple_of(table[1, t] * BS, BS), BS)
                pltpu.make_async_copy(place.at[:, rows, :], out.at[t], sem.at[t]).start()

    for t in range(FAR):

        @pl.when(table[0, t] < 8)
        def _():
            pltpu.make_async_copy(places[0].at[:, pl.ds(0, BS), :], out.at[t], sem.at[t]).wait()


def pick(table, places):
    return pl.pallas_call(
        pick_kernel,
        out_shape=jax.ShapeDtypeStruct((FAR, 2, BS, D), BF),
        in_specs=[SMEM] + [HBM] * 8,
        out_specs=VMEM,
        scratch_shapes=[pltpu.SemaphoreType.DMA((FAR,))],
        compiler_params=pltpu.CompilerParams(vmem_limit_bytes=4 * 2**20),
        cost_estimate=pl.CostEstimate(flops=0, bytes_accessed=6 * 2**20, transcendentals=0),
    )(table, *places)


def offer_kernel(table, keys, values, *refs):
    outs, sem = refs[:2], refs[2]
    copies = []
    for t in range(2 * W):
        rows = pl.ds(pl.multiple_of(table[t] * BS, BS), BS)
        for half, source in enumerate((keys, values)):
            target = outs[t // W].at[t % W, half]
            copies.append(pltpu.make_async_copy(source.at[rows, :], target, sem.at[t, half]))
    for copy in copies:
        copy.start()
    for copy in copies:
        copy.wait()


def offer(table, keys, values):
    return pl.pallas_call(
        offer_kernel,
        out_shape=(jax.ShapeDtypeStruct((W, 2, BS, D), BF),) * 2,
        in_specs=[SMEM, HBM, HBM],
        out_specs=(VMEM,) * 2,
        scratch_shapes=[pltpu.SemaphoreType.DMA((2 * W, 2))],
        compiler_params=pltpu.CompilerParams(vmem_limit_bytes=4 * 2**20),
        cost_estimate=pl.CostEstimate(flops=0, bytes_accessed=2 * 2**20, transcendentals=0),
    )(table, keys, values)


def attend_pair(step, table, q_ref, g_ref, listed, att_ref, gq_ref, totals):
    low = lax.broadcasted_iota(jnp.int32, (BS, 128), 1) < 64
    last = (((1,), (1,)), ((), ()))
    first = (((0,), (0,)), ((), ()))
    s = step // PAIRS
    p = step % PAIRS
    cols = pl.ds(pl.multiple_of(p * 128, 128), 128)
    query = q_ref[s, :, cols]
    grad = g_ref[s, :, cols]
    zero = jnp.zeros_like(query)
    query2 = jnp.concatenate([jnp.where(low, query, zero), jnp.where(low, zero, query)], axis=0)
    grad2 = jnp.concatenate([jnp.where(low, grad, zero), jnp.where(low, zero, grad)], axis=0)
    keys = listed[s, 0, :, cols]
    values = listed[s, 1, :, cols]

    def own_heads(both):
        return jnp.concatenate([both[:64, :128], both[64:, 128:]], axis=0)

    scores = lax.dot_general(keys, query2, last, preferred_element_type=F32)
    grad_weights = lax.dot_general(values, grad2, last, preferred_element_type=F32)
    highest = jnp.max(scores, axis=0, keepdims=True)
    raised = jnp.exp2((scores - highest) * (0.125 * math.log2(math.e)))
    weights = raised * (1.0 / jnp.sum(raised, axis=0, keepdims=True))
    weights_low = weights.astype(BF)
    grad_value = jnp.dot(weights_low, grad2, preferred_element_type=F32)
    mixture = own_heads(lax.dot_general(values, weights_low, first, preferred_element_type=F32))
    att_ref[s, :, cols] = mixture.T.astype(BF)
    product = mixture * grad.astype(F32).T
    carried = jnp.concatenate(
        [jnp.sum(product[:64], axis=0, keepdims=True), jnp.sum(product[64:], axis=0, keepdims=True)], axis=1
    )
    grad_scores = ((weights * (grad_weights - carried)) * 0.125).astype(BF)
    grad_query = own_heads(lax.dot_general(keys, grad_scores, first, preferred_element_type=F32))
    gq_ref[s, :, cols] = grad_query.T.astype(BF)
    grad_key = jnp.dot(grad_scores, query2, preferred_element_type=F32)
    for j in range(KB):
        slot = table[2, s * KB + j]
        again = table[3, s * KB + j] == 0
        rows = slice(j * BS, (j + 1) * BS)
        for half, term in enumerate((grad_key, grad_value)):
            before = totals[slot, half, :, cols]
            totals[slot, half, :, cols] = jnp.where(again, before, 0.0) + term[rows]


def attend_kernel(table, q_ref, g_ref, *refs):
    own, (one, two, other), places, picked = refs[0], refs[1:4], refs[4:12], refs[12]
    near = (one.at[0], two.at[0], other.at[0], other.at[1])
    att_ref, gq_ref, own_out, far_out, keep_out, give_out, listed, totals, sem = refs[13:]

    def bring(source, s, j):
        pltpu.make_async_copy(source, listed.at[s, :, pl.ds(j * BS, BS), :], sem.at[s]).start()

    for s in range(NB):
        bring(own.at[:, pl.ds(s * BS, BS), :], s, 0)
        for j in range(1, KB):
            code, place = table[0, s * KB + j], table[1, s * KB + j]
            rows = pl.ds(pl.multiple_of(place * BS, BS), BS)
            if j <= LOC:

                @pl.when(code == 0)
                def _():
                    bring(own.at[:, rows, :], s, j)

                for t in range(2 * W):

                    @pl.when(code == 1 + t)
                    def _():
                        bring(near[t], s, j)

            else:
                for t in range(8):

                    @pl.when(code == t)
                    def _():
                        bring(places[t].at[:, rows, :], s, j)

                @pl.when(code == 8)
                def _():
                    bring(picked.at[s * EXP + j - 1 - LOC], s, j)

    def body(step, carry):
        attend_pair(step, table, q_ref, g_ref, listed, att_ref, gq_ref, totals)
        return carry

    for s in range(NB):
        pltpu.make_async_copy(listed.at[s], listed.at[s], sem.at[s]).wait()

    def body(step, carry):
        attend_pair(step, table, q_ref, g_ref, listed, att_ref, gq_ref, totals)
        return carry

    lax.fori_loop(0, NB * PAIRS, body, 0, unroll=PAIRS)
    own_out[...] = totals[:NB].astype(BF)
    keep_out[...] = totals[NB : NB + W].astype(BF)
    give_out[...] = totals[NB + W : NEAR].astype(BF)
    far_out[...] = totals[NEAR:].astype(BF)


def attend(table, queries, cotangent, own, near, places, picked):
    return pl.pallas_call(
        attend_kernel,
        out_shape=(
            jax.ShapeDtypeStruct((NB, BS, D), BF),
            jax.ShapeDtypeStruct((NB, BS, D), BF),
            jax.ShapeDtypeStruct((NB, 2, BS, D), BF),
            jax.ShapeDtypeStruct((FAR, 2, BS, D), BF),
        )
        + (jax.ShapeDtypeStruct((W, 2, BS, D), BF),) * 2,
        in_specs=[SMEM, VMEM, VMEM] + [HBM] * 13,
        out_specs=(VMEM,) * 6,
        scratch_shapes=[
            pltpu.VMEM((NB, 2, ROWS, D), BF),
            pltpu.VMEM((NEAR + FAR, 2, BS, D), F32),
            pltpu.SemaphoreType.DMA((NB,)),
        ],
        compiler_params=pltpu.CompilerParams(vmem_limit_bytes=32 * 2**20),
        cost_estimate=pl.CostEstimate(
            flops=12 * NB * BS * ROWS * D, bytes_accessed=12 * 2**20, transcendentals=NB * 8 * BS * ROWS
        ),
    )(table, queries, cotangent, own, *near, *places, picked)


def spread_kernel(count, table, mine, theirs, *outs):
    for n in range(count):
        out = outs[n]
        for s in range(NB):
            a, b = table[0, n * NB + s], table[1, n * NB + s]

            @pl.when((a < 0) & (b < 0))
            def _():
                out[s] = jnp.zeros((2, BS, D), BF)

            @pl.when((a >= 0) & (b < 0))
            def _():
                out[s] = mine[a]

            @pl.when((a < 0) & (b >= 0))
            def _():
                out[s] = theirs[b]

            @pl.when((a >= 0) & (b >= 0))
            def _():
                out[s] = (mine[a].astype(F32) + theirs[b].astype(F32)).astype(BF)


def spread(table, mine, theirs):
    count = table.shape[1] // NB
    return pl.pallas_call(
        functools.partial(spread_kernel, count),
        out_shape=tuple(jax.ShapeDtypeStruct((NB, 2, BS, D), BF) for _ in range(count)),
        in_specs=[SMEM, VMEM, VMEM],
        out_specs=(VMEM,) * count,
        compiler_params=pltpu.CompilerParams(vmem_limit_bytes=12 * 2**20),
        cost_estimate=pl.CostEstimate(flops=0, bytes_accessed=(3 + count) * 2**19, transcendentals=0),
    )(table, mine, theirs)


def close_kernel(table, near, theirs, from_a, from_b, *refs):
    (one, two, other), (gk_ref, gv_ref) = refs[:3], refs[3:]
    returned = (one.at[0], two.at[0], other.at[0], other.at[1])
    for s in range(NB):
        for half, out in enumerate((gk_ref, gv_ref)):
            total = near[s, half].astype(F32)
            for t in range(2 * W):
                total = total + jnp.where(table[t] == s, returned[t][half].astype(F32), 0.0)
            total = total + from_a[s, half].astype(F32) + from_b[s, half].astype(F32)
            b = table[4 + s]
            direct = theirs[jnp.maximum(b, 0), half].astype(F32)
            total = total + jnp.where(b >= 0, direct, 0.0)
            out[pl.ds(s * BS, BS), :] = total.astype(BF)


def close(table, near, theirs, from_a, from_b, returned):
    return pl.pallas_call(
        close_kernel,
        out_shape=(jax.ShapeDtypeStruct((NB * BS, D), BF),) * 2,
        in_specs=[SMEM] + [VMEM] * 7,
        out_specs=(VMEM, VMEM),
        compiler_params=pltpu.CompilerParams(vmem_limit_bytes=12 * 2**20),
        cost_estimate=pl.CostEstimate(flops=2**22, bytes_accessed=6 * 2**20, transcendentals=0),
    )(table, near, theirs, from_a, from_b, *returned)


def on_device(queries, keys, values, cotangent, local_list, far_list):
    groups = lax.axis_size("group")
    doms = lax.axis_size("dom")
    chips = groups // 2
    dom = lax.axis_index("dom").astype(jnp.int32)
    group = lax.axis_index("group").astype(jnp.int32)
    chip, core = group // 2, group % 2
    i32 = jnp.int32

    own = jnp.stack([keys, values])
    flow_a = [ring_step(own)]
    sibling = swap_cores(own)

    padded = jnp.pad(local_list, ((W * NB, W * NB), (0, 0)), constant_values=-1)
    around = lax.dynamic_slice_in_dim(padded, dom * NB, (2 * W + 1) * NB, 0).reshape(2 * W + 1, NB * LOC)
    given = jnp.max(jnp.where(around // NB == dom, around % NB, 0), axis=1).astype(i32)
    up, down = given[W + 1 :], given[:W][::-1]
    given = jnp.where(core == 0, jnp.concatenate([up, down]), jnp.concatenate([down, up]))
    local = around[W].reshape(NB, LOC)
    holder = local // NB - dom
    direct = (holder < 0) == (core == 0)
    near_code = jnp.where(holder == 0, 0, jnp.abs(holder) + jnp.where(direct, 0, W))
    near_key = jnp.where(holder == 0, local % NB, NB - 1 + near_code)

    far_rows = far_list[0].reshape(groups, FAR)
    mine = lax.dynamic_index_in_dim(far_rows, group, 0, keepdims=False)
    theirs = lax.dynamic_index_in_dim(far_rows, group ^ 1, 0, keepdims=False)
    far_code = place_of(mine // NB, chip, core, chips)
    needed = place_of(theirs // NB, chip, 1 - core, chips) == PICKED
    sent = jnp.where(needed, place_of(theirs // NB, chip, core, chips), PICKED)
    pick_table = jnp.stack([sent, theirs % NB]).astype(i32)

    self_code = jnp.zeros((NB, 1), i32)
    self_key = jnp.arange(NB, dtype=i32)[:, None]
    codes = jnp.concatenate([self_code, near_code, far_code.reshape(NB, EXP)], axis=1).reshape(-1)
    slots = jnp.concatenate([self_key, local % NB, (mine % NB).reshape(NB, EXP)], axis=1).reshape(-1)
    far_key = (NEAR + first_of(mine)).reshape(NB, EXP)
    targets = jnp.concatenate([self_key, near_key, far_key], axis=1).reshape(-1)
    leads = first_of(targets) == jnp.arange(ENTRIES, dtype=i32)
    table = jnp.stack([codes, slots, targets, leads.astype(i32)]).astype(i32)
    steps = [(4, 0), (3, 1), (3, 0), (2, 1), (2, 0), (1, 1), (1, 0)]
    direction = 1 - 2 * core
    wanted = []
    for distance, side in steps:
        cluster = ((chip + direction * distance) % chips) * 2 + jnp.where(side == 0, core, 1 - core)
        wanted += [cluster * NB, cluster * NB + 1]
    wanted += [group * NB, group * NB + 1]
    wanted = jnp.stack(wanted).astype(i32)
    hits = jnp.stack([slot_in(mine, wanted), slot_in(theirs, wanted)])
    last = jnp.concatenate([given, hits[1, 7 * NB :]]).astype(i32)
    tables = (given, pick_table, table, hits[:, : 2 * NB], hits[:, 2 * NB : 7 * NB], last)
    sibling, tables = lax.optimization_barrier((sibling, tables))
    flow_b = [ring_step(sibling)]
    given, pick_table, table, hits_first, hits_rest, last = tables

    flow_a.append(ring_step(flow_a[0]))
    keep, give = offer(given, keys, values)
    given_here = swap_cores(give)
    two = dom_step(jnp.stack([keep[1], given_here[1]]), 2)
    flow_b[0], two = lax.optimization_barrier((flow_b[0], two))
    flow_b.append(ring_step(flow_b[0]))
    flow_a.append(ring_step(flow_a[1]))
    flow_b.append(ring_step(flow_b[1]))
    keep, given_here, two = lax.optimization_barrier((keep, given_here, two))
    one = dom_step(jnp.stack([keep[0], given_here[0]]), 1)
    flow_a.append(ring_step(flow_a[2]))
    flow_a[3], one = lax.optimization_barrier((flow_a[3], one))
    near = (one, two, swap_cores(jnp.stack([one[1], two[1]])))

    picked = swap_cores(pick(pick_table, [sibling] + flow_a + flow_b))
    attended, grad_queries, own_terms, far_terms, keep, give = attend(
        table,
        queries.reshape(NB, BS, D),
        cotangent.reshape(NB, BS, D),
        own,
        near,
        [sibling] + flow_a + flow_b,
        picked,
    )

    sibling_terms = swap_cores(far_terms)
    sibling_terms, give = lax.optimization_barrier((sibling_terms, give))
    start_a, start_b = spread(hits_first, far_terms, sibling_terms)
    a3, b2, a2, b1, a1 = spread(hits_rest, far_terms, sibling_terms)

    def joined(x, y):
        return (x.astype(F32) + y.astype(F32)).astype(BF)

    back_a = ring_step(start_a)
    back_b = ring_step(start_b)
    given_here = swap_cores(give)
    back_a = ring_step(joined(back_a, a3))
    two = dom_step(jnp.stack([keep[1], given_here[1]]), -2)
    back_b = ring_step(joined(back_b, b2))
    back_a = ring_step(joined(back_a, a2))
    back_b, two = lax.optimization_barrier((back_b, two))
    back_b = ring_step(joined(back_b, b1))
    keep, given_here, two = lax.optimization_barrier((keep, given_here, two))
    one = dom_step(jnp.stack([keep[0], given_here[0]]), -1)
    back_a = ring_step(joined(back_a, a1))
    other, back_b = lax.optimization_barrier((jnp.stack([one[1], two[1]]), back_b))
    back_b = swap_cores(back_b)
    returned = (one, two, swap_cores(other))

    grad_keys, grad_values = close(last, own_terms, sibling_terms, back_a, back_b, returned)
    return (attended.reshape(NB * BS, D), grad_queries.reshape(NB * BS, D), grad_keys, grad_values)


def solution(mesh):
    rows = P(("group", "dom"), None)
    return jax.shard_map(
        on_device,
        mesh=mesh,
        in_specs=(rows, rows, rows, rows, P("group", None), P("dom", None, None)),
        out_specs=(rows, rows, rows, rows),
        check_vma=False,
    )
```

```python
import functools
import math

import jax
import jax.numpy as jnp
from jax import lax
from jax.experimental import pallas as pl
from jax.experimental.pallas import tpu as pltpu
from jax.sharding import PartitionSpec as P

D = 512
BS = 128
NB = 2
LOC = 3
EXP = 3
W = 2
KB = 1 + LOC + EXP
ENTRIES = NB * KB
ROWS = KB * BS
FAR = NB * EXP
NEAR = NB + 2 * W
PAIRS = D // 128
BF = jnp.bfloat16
F32 = jnp.float32

HBM = pl.BlockSpec(memory_space=pltpu.HBM)
VMEM = pl.BlockSpec(memory_space=pltpu.VMEM)
SMEM = pl.BlockSpec(memory_space=pltpu.SMEM)

SIBLING, FLOW_A, FLOW_B, PICKED = 0, 0, 4, 8


def ring_step(array):
    size = lax.axis_size("group")
    return lax.ppermute(array, "group", [(g, (g + (2 if g % 2 == 0 else -2)) % size) for g in range(size)])


def swap_cores(array):
    size = lax.axis_size("group")
    return lax.ppermute(array, "group", [(g, g ^ 1) for g in range(size)])


def dom_step(array, by):
    groups, doms = lax.axis_size("group"), lax.axis_size("dom")
    pairs = []
    for g in range(groups):
        for i in range(doms):
            to = i + (by if g % 2 == 0 else -by)
            if 0 <= to < doms:
                pairs.append((g * doms + i, g * doms + to))
    return lax.ppermute(array, ("group", "dom"), pairs)


def place_of(cluster, chip, core, chips):
    other_chip, other_core = cluster // 2, cluster % 2
    distance = jnp.where(core == 0, chip - other_chip, other_chip - chip) % chips
    same = other_core == core
    half = chips // 2
    here = jnp.where(same, FLOW_A + distance, FLOW_B + distance)
    held = jnp.where(same, distance <= half, distance < half)
    return jnp.where(distance == 0, SIBLING, jnp.where(held, here, PICKED))


def first_of(values):
    order = jnp.arange(values.shape[0], dtype=jnp.int32)
    same = values[:, None] == values[None, :]
    return jnp.min(jnp.where(same, order[None, :], values.shape[0]), axis=1)


def slot_in(values, wanted):
    order = jnp.arange(values.shape[0], dtype=jnp.int32)
    hit = values[None, :] == wanted[:, None]
    found = jnp.min(jnp.where(hit, order[None, :], values.shape[0]), axis=1)
    return jnp.where(found == values.shape[0], -1, found).astype(jnp.int32)


def pick_kernel(table, *refs):
    places, out, sem = refs[:8], refs[8], refs[9]
    copies = []
    for t in range(FAR):
        for code, place in enumerate(places):

            @pl.when(table[0, t] == code)
            def _():
                rows = pl.ds(pl.multiple_of(table[1, t] * BS, BS), BS)
                pltpu.make_async_copy(place.at[:, rows, :], out.at[t], sem.at[t]).start()

    for t in range(FAR):

        @pl.when(table[0, t] < 8)
        def _():
            pltpu.make_async_copy(places[0].at[:, pl.ds(0, BS), :], out.at[t], sem.at[t]).wait()


def pick(table, places):
    return pl.pallas_call(
        pick_kernel,
        out_shape=jax.ShapeDtypeStruct((FAR, 2, BS, D), BF),
        in_specs=[SMEM] + [HBM] * 8,
        out_specs=VMEM,
        scratch_shapes=[pltpu.SemaphoreType.DMA((FAR,))],
        compiler_params=pltpu.CompilerParams(vmem_limit_bytes=4 * 2**20),
        cost_estimate=pl.CostEstimate(flops=0, bytes_accessed=6 * 2**20, transcendentals=0),
    )(table, *places)


def offer_kernel(table, keys, values, *refs):
    outs, sem = refs[:2], refs[2]
    copies = []
    for t in range(2 * W):
        rows = pl.ds(pl.multiple_of(table[t] * BS, BS), BS)
        for half, source in enumerate((keys, values)):
            target = outs[t // W].at[t % W, half]
            copies.append(pltpu.make_async_copy(source.at[rows, :], target, sem.at[t, half]))
    for copy in copies:
        copy.start()
    for copy in copies:
        copy.wait()


def offer(table, keys, values):
    return pl.pallas_call(
        offer_kernel,
        out_shape=(jax.ShapeDtypeStruct((W, 2, BS, D), BF),) * 2,
        in_specs=[SMEM, HBM, HBM],
        out_specs=(VMEM,) * 2,
        scratch_shapes=[pltpu.SemaphoreType.DMA((2 * W, 2))],
        compiler_params=pltpu.CompilerParams(vmem_limit_bytes=4 * 2**20),
        cost_estimate=pl.CostEstimate(flops=0, bytes_accessed=2 * 2**20, transcendentals=0),
    )(table, keys, values)


def attend_pair(step, table, q_ref, g_ref, listed, att_ref, gq_ref, totals):
    low = lax.broadcasted_iota(jnp.int32, (BS, 128), 1) < 64
    last = (((1,), (1,)), ((), ()))
    first = (((0,), (0,)), ((), ()))
    s = step // PAIRS
    p = step % PAIRS
    cols = pl.ds(pl.multiple_of(p * 128, 128), 128)
    query = q_ref[s, :, cols]
    grad = g_ref[s, :, cols]
    zero = jnp.zeros_like(query)
    query2 = jnp.concatenate([jnp.where(low, query, zero), jnp.where(low, zero, query)], axis=0)
    grad2 = jnp.concatenate([jnp.where(low, grad, zero), jnp.where(low, zero, grad)], axis=0)
    keys = listed[s, 0, :, cols]
    values = listed[s, 1, :, cols]

    def own_heads(both):
        return jnp.concatenate([both[:64, :128], both[64:, 128:]], axis=0)

    scores = lax.dot_general(keys, query2, last, preferred_element_type=F32)
    grad_weights = lax.dot_general(values, grad2, last, preferred_element_type=F32)
    highest = jnp.max(scores, axis=0, keepdims=True)
    raised = jnp.exp2((scores - highest) * (0.125 * math.log2(math.e)))
    weights = raised * (1.0 / jnp.sum(raised, axis=0, keepdims=True))
    weights_low = weights.astype(BF)
    grad_value = jnp.dot(weights_low, grad2, preferred_element_type=F32)
    mixture = own_heads(lax.dot_general(values, weights_low, first, preferred_element_type=F32))
    att_ref[s, :, cols] = mixture.T.astype(BF)
    product = mixture * grad.astype(F32).T
    carried = jnp.concatenate(
        [jnp.sum(product[:64], axis=0, keepdims=True), jnp.sum(product[64:], axis=0, keepdims=True)], axis=1
    )
    grad_scores = ((weights * (grad_weights - carried)) * 0.125).astype(BF)
    grad_query = own_heads(lax.dot_general(keys, grad_scores, first, preferred_element_type=F32))
    gq_ref[s, :, cols] = grad_query.T.astype(BF)
    grad_key = jnp.dot(grad_scores, query2, preferred_element_type=F32)
    for j in range(KB):
        slot = table[2, s * KB + j]
        again = table[3, s * KB + j] == 0
        rows = slice(j * BS, (j + 1) * BS)
        for half, term in enumerate((grad_key, grad_value)):
            before = totals[slot, half, :, cols]
            totals[slot, half, :, cols] = jnp.where(again, before, 0.0) + term[rows]


def attend_kernel(table, q_ref, g_ref, *refs):
    own, (one, two, other), places, picked = refs[0], refs[1:4], refs[4:12], refs[12]
    near = (one.at[0], two.at[0], other.at[0], other.at[1])
    att_ref, gq_ref, own_out, far_out, keep_out, give_out, listed, totals, sem = refs[13:]

    def bring(source, s, j):
        pltpu.make_async_copy(source, listed.at[s, :, pl.ds(j * BS, BS), :], sem.at[s]).start()

    for s in range(NB):
        bring(own.at[:, pl.ds(s * BS, BS), :], s, 0)
        for j in range(1, KB):
            code, place = table[0, s * KB + j], table[1, s * KB + j]
            rows = pl.ds(pl.multiple_of(place * BS, BS), BS)
            if j <= LOC:

                @pl.when(code == 0)
                def _():
                    bring(own.at[:, rows, :], s, j)

                for t in range(2 * W):

                    @pl.when(code == 1 + t)
                    def _():
                        bring(near[t], s, j)

            else:
                for t in range(8):

                    @pl.when(code == t)
                    def _():
                        bring(places[t].at[:, rows, :], s, j)

                @pl.when(code == 8)
                def _():
                    bring(picked.at[s * EXP + j - 1 - LOC], s, j)

    def body(step, carry):
        attend_pair(step, table, q_ref, g_ref, listed, att_ref, gq_ref, totals)
        return carry

    for s in range(NB):
        pltpu.make_async_copy(listed.at[s], listed.at[s], sem.at[s]).wait()

    def body(step, carry):
        attend_pair(step, table, q_ref, g_ref, listed, att_ref, gq_ref, totals)
        return carry

    lax.fori_loop(0, NB * PAIRS, body, 0, unroll=PAIRS)
    own_out[...] = totals[:NB].astype(BF)
    keep_out[...] = totals[NB : NB + W].astype(BF)
    give_out[...] = totals[NB + W : NEAR].astype(BF)
    far_out[...] = totals[NEAR:].astype(BF)


def attend(table, queries, cotangent, own, near, places, picked):
    return pl.pallas_call(
        attend_kernel,
        out_shape=(
            jax.ShapeDtypeStruct((NB, BS, D), BF),
            jax.ShapeDtypeStruct((NB, BS, D), BF),
            jax.ShapeDtypeStruct((NB, 2, BS, D), BF),
            jax.ShapeDtypeStruct((FAR, 2, BS, D), BF),
        )
        + (jax.ShapeDtypeStruct((W, 2, BS, D), BF),) * 2,
        in_specs=[SMEM, VMEM, VMEM] + [HBM] * 13,
        out_specs=(VMEM,) * 6,
        scratch_shapes=[
            pltpu.VMEM((NB, 2, ROWS, D), BF),
            pltpu.VMEM((NEAR + FAR, 2, BS, D), F32),
            pltpu.SemaphoreType.DMA((NB,)),
        ],
        compiler_params=pltpu.CompilerParams(vmem_limit_bytes=32 * 2**20),
        cost_estimate=pl.CostEstimate(
            flops=12 * NB * BS * ROWS * D, bytes_accessed=12 * 2**20, transcendentals=NB * 8 * BS * ROWS
        ),
    )(table, queries, cotangent, own, *near, *places, picked)


def spread_kernel(count, table, mine, theirs, *outs):
    for n in range(count):
        out = outs[n]
        for s in range(NB):
            a, b = table[0, n * NB + s], table[1, n * NB + s]

            @pl.when((a < 0) & (b < 0))
            def _():
                out[s] = jnp.zeros((2, BS, D), BF)

            @pl.when((a >= 0) & (b < 0))
            def _():
                out[s] = mine[a]

            @pl.when((a < 0) & (b >= 0))
            def _():
                out[s] = theirs[b]

            @pl.when((a >= 0) & (b >= 0))
            def _():
                out[s] = (mine[a].astype(F32) + theirs[b].astype(F32)).astype(BF)


def spread(table, mine, theirs):
    count = table.shape[1] // NB
    return pl.pallas_call(
        functools.partial(spread_kernel, count),
        out_shape=tuple(jax.ShapeDtypeStruct((NB, 2, BS, D), BF) for _ in range(count)),
        in_specs=[SMEM, VMEM, VMEM],
        out_specs=(VMEM,) * count,
        compiler_params=pltpu.CompilerParams(vmem_limit_bytes=12 * 2**20),
        cost_estimate=pl.CostEstimate(flops=0, bytes_accessed=(3 + count) * 2**19, transcendentals=0),
    )(table, mine, theirs)


def close_kernel(table, near, theirs, from_a, from_b, *refs):
    (one, two, other), (gk_ref, gv_ref) = refs[:3], refs[3:]
    returned = (one.at[0], two.at[0], other.at[0], other.at[1])
    for s in range(NB):
        for half, out in enumerate((gk_ref, gv_ref)):
            total = near[s, half].astype(F32)
            for t in range(2 * W):
                total = total + jnp.where(table[t] == s, returned[t][half].astype(F32), 0.0)
            total = total + from_a[s, half].astype(F32) + from_b[s, half].astype(F32)
            b = table[4 + s]
            direct = theirs[jnp.maximum(b, 0), half].astype(F32)
            total = total + jnp.where(b >= 0, direct, 0.0)
            out[pl.ds(s * BS, BS), :] = total.astype(BF)


def close(table, near, theirs, from_a, from_b, returned):
    return pl.pallas_call(
        close_kernel,
        out_shape=(jax.ShapeDtypeStruct((NB * BS, D), BF),) * 2,
        in_specs=[SMEM] + [VMEM] * 7,
        out_specs=(VMEM, VMEM),
        compiler_params=pltpu.CompilerParams(vmem_limit_bytes=12 * 2**20),
        cost_estimate=pl.CostEstimate(flops=2**22, bytes_accessed=6 * 2**20, transcendentals=0),
    )(table, near, theirs, from_a, from_b, *returned)


def on_device(queries, keys, values, cotangent, local_list, far_list):
    groups = lax.axis_size("group")
    doms = lax.axis_size("dom")
    chips = groups // 2
    dom = lax.axis_index("dom").astype(jnp.int32)
    group = lax.axis_index("group").astype(jnp.int32)
    chip, core = group // 2, group % 2
    i32 = jnp.int32

    own = jnp.stack([keys, values])
    flow_a = [ring_step(own)]
    sibling = swap_cores(own)

    padded = jnp.pad(local_list, ((W * NB, W * NB), (0, 0)), constant_values=-1)
    around = lax.dynamic_slice_in_dim(padded, dom * NB, (2 * W + 1) * NB, 0).reshape(2 * W + 1, NB * LOC)
    given = jnp.max(jnp.where(around // NB == dom, around % NB, 0), axis=1).astype(i32)
    up, down = given[W + 1 :], given[:W][::-1]
    given = jnp.where(core == 0, jnp.concatenate([up, down]), jnp.concatenate([down, up]))
    local = around[W].reshape(NB, LOC)
    holder = local // NB - dom
    direct = (holder < 0) == (core == 0)
    near_code = jnp.where(holder == 0, 0, jnp.abs(holder) + jnp.where(direct, 0, W))
    near_key = jnp.where(holder == 0, local % NB, NB - 1 + near_code)

    far_rows = far_list[0].reshape(groups, FAR)
    mine = lax.dynamic_index_in_dim(far_rows, group, 0, keepdims=False)
    theirs = lax.dynamic_index_in_dim(far_rows, group ^ 1, 0, keepdims=False)
    far_code = place_of(mine // NB, chip, core, chips)
    needed = place_of(theirs // NB, chip, 1 - core, chips) == PICKED
    sent = jnp.where(needed, place_of(theirs // NB, chip, core, chips), PICKED)
    pick_table = jnp.stack([sent, theirs % NB]).astype(i32)

    self_code = jnp.zeros((NB, 1), i32)
    self_key = jnp.arange(NB, dtype=i32)[:, None]
    codes = jnp.concatenate([self_code, near_code, far_code.reshape(NB, EXP)], axis=1).reshape(-1)
    slots = jnp.concatenate([self_key, local % NB, (mine % NB).reshape(NB, EXP)], axis=1).reshape(-1)
    far_key = (NEAR + first_of(mine)).reshape(NB, EXP)
    targets = jnp.concatenate([self_key, near_key, far_key], axis=1).reshape(-1)
    leads = first_of(targets) == jnp.arange(ENTRIES, dtype=i32)
    table = jnp.stack([codes, slots, targets, leads.astype(i32)]).astype(i32)
    steps = [(4, 0), (3, 1), (3, 0), (2, 1), (2, 0), (1, 1), (1, 0)]
    direction = 1 - 2 * core
    wanted = []
    for distance, side in steps:
        cluster = ((chip + direction * distance) % chips) * 2 + jnp.where(side == 0, core, 1 - core)
        wanted += [cluster * NB, cluster * NB + 1]
    wanted += [group * NB, group * NB + 1]
    wanted = jnp.stack(wanted).astype(i32)
    hits = jnp.stack([slot_in(mine, wanted), slot_in(theirs, wanted)])
    last = jnp.concatenate([given, hits[1, 7 * NB :]]).astype(i32)
    tables = (pick_table, table, hits[:, : 2 * NB], hits[:, 2 * NB : 7 * NB], last)
    sibling, given = lax.optimization_barrier((sibling, given))
    flow_b = [ring_step(sibling)]

    flow_a.append(ring_step(flow_a[0]))
    keep, give = offer(given, keys, values)
    given_here = swap_cores(give)
    two = dom_step(jnp.stack([keep[1], given_here[1]]), 2)
    flow_b[0], two, tables = lax.optimization_barrier((flow_b[0], two, tables))
    pick_table, table, hits_first, hits_rest, last = tables
    flow_b.append(ring_step(flow_b[0]))
    flow_a.append(ring_step(flow_a[1]))
    flow_b.append(ring_step(flow_b[1]))
    keep, given_here, two = lax.optimization_barrier((keep, given_here, two))
    one = dom_step(jnp.stack([keep[0], given_here[0]]), 1)
    flow_a.append(ring_step(flow_a[2]))
    flow_a[3], one = lax.optimization_barrier((flow_a[3], one))
    near = (one, two, swap_cores(jnp.stack([one[1], two[1]])))

    picked = swap_cores(pick(pick_table, [sibling] + flow_a + flow_b))
    attended, grad_queries, own_terms, far_terms, keep, give = attend(
        table,
        queries.reshape(NB, BS, D),
        cotangent.reshape(NB, BS, D),
        own,
        near,
        [sibling] + flow_a + flow_b,
        picked,
    )

    sibling_terms = swap_cores(far_terms)
    sibling_terms, give = lax.optimization_barrier((sibling_terms, give))
    start_a, start_b = spread(hits_first, far_terms, sibling_terms)
    a3, b2, a2, b1, a1 = spread(hits_rest, far_terms, sibling_terms)

    def joined(x, y):
        return (x.astype(F32) + y.astype(F32)).astype(BF)

    back_a = ring_step(start_a)
    back_b = ring_step(start_b)
    given_here = swap_cores(give)
    back_a = ring_step(joined(back_a, a3))
    two = dom_step(jnp.stack([keep[1], given_here[1]]), -2)
    back_b = ring_step(joined(back_b, b2))
    back_a = ring_step(joined(back_a, a2))
    back_b, two = lax.optimization_barrier((back_b, two))
    back_b = ring_step(joined(back_b, b1))
    keep, given_here, two = lax.optimization_barrier((keep, given_here, two))
    one = dom_step(jnp.stack([keep[0], given_here[0]]), -1)
    back_a = ring_step(joined(back_a, a1))
    other, back_b = lax.optimization_barrier((jnp.stack([one[1], two[1]]), back_b))
    back_b = swap_cores(back_b)
    returned = (one, two, swap_cores(other))

    grad_keys, grad_values = close(last, own_terms, sibling_terms, back_a, back_b, returned)
    return (attended.reshape(NB * BS, D), grad_queries.reshape(NB * BS, D), grad_keys, grad_values)


def solution(mesh):
    rows = P(("group", "dom"), None)
    return jax.shard_map(
        on_device,
        mesh=mesh,
        in_specs=(rows, rows, rows, rows, P("group", None), P("dom", None, None)),
        out_specs=(rows, rows, rows, rows),
        check_vma=False,
    )
```
